1024 devices in a mesh: dp: 32 (over z, y_hi), expert: 32 (over x, y_lo, core).
Axes of the slice: x: 8, y: 8 (y_hi: 4, y_lo: 2; y = y_hi * 2 + y_lo), z: 8, core: 2. Of those that a mesh axis runs over, the one named last changes fastest.
Arguments:
- tokens: bfloat16 [131072, 1280], P(('dp', 'expert')), may hold values from -6 to 6
- routes: int32 [131072, 1], P(('dp', 'expert')), may hold values from 0 to 15
- pool_ids: int32 [32, 4096], P('dp', 'expert'), may hold values from 0 to 7, never falling along the last dimension, each value on 1 to 1024 neighbouring positions
- w_router: bfloat16 [1280, 16], replicated, may hold values from -0.15625 to 0.15625
- w_up: bfloat16 [1280, 40960], P(None, 'expert'), may hold values from -0.15625 to 0.15625
- w_down: bfloat16 [40960, 1280], P('expert'), may hold values from -0.125 to 0.125
- captions: bfloat16 [256, 1280], P('dp'), may hold values from -6 to 6
- clip_pairs: int32 [256], replicated, may hold values from 0 to 255, each once
- teacher: float32 [256, 256], P('dp'), may hold values from -12 to 12
Outputs:
- token_grads: float32 [131072, 1280], P(('dp', 'expert'))
- caption_grads: float32 [256, 1280], P('dp')
The draws below stay inside these ranges and needn't reach their ends.
Inputs may be any that keep to these rules, and one draw needn't show every extreme that they name: `pool_ids`: within each index of dp the clip numbers never fall along the tokens, and every clip has 1 to 1024 tokens. `clip_pairs`: each clip is named by exactly one caption.
All inputs are finite; a program needn't handle non-finite values.
Results may differ from the reference program's by a relative error of at most 0.0018.
Values may be sent and summed in bfloat16 or wider, within the bound.
No kernel may reach another device: no remote copies, remote signals or barrier semaphores. Data moves between devices by JAX's collectives and lax.ppermute only.
A program may use at most 64 MiB of HBM per device.

```python
import math
import jax
import jax.numpy as jnp
import numpy as np
from jax import lax

D = 1280
FFW = 2560
TOK_DEV = 128
CLIPS_G = 8
EXPERTS = 16
SLOT = 8
GROUP_TOK = 4096
TOKENS = 131072
CAPS = 256
CLIP_MOST = 1024
N_DP = 32
N_EXPERT = 32


def level_of(key, extent, split, least, top_value):
    level, own = 1.0, jax.random.fold_in(key, 6)
    for axis_at, parts in split:
        steps = jnp.exp(jax.random.uniform(jax.random.fold_in(own, axis_at), (parts,), jnp.float32, least / len(split), top_value / len(split)))
        level = level * jnp.repeat(steps, extent[axis_at] // parts).reshape([-1 if axis == axis_at else 1 for axis in range(len(extent))])
    return level


def picks_of(key, rows, count, top, lift):
    ranking = jax.random.permutation(jax.random.fold_in(key, 1), count)
    boost = ranking
    for power in range(3):
        boost = boost * boost // count
    boost = boost * lift // count
    chance = jax.random.randint(jax.random.fold_in(key, 2), (rows, count), 0, 4096) + boost
    holders = jax.random.permutation(jax.random.fold_in(key, 3), rows)[jnp.arange(count) % rows]
    chance = jnp.where(jnp.arange(rows)[:, None] == holders[None, :], 1 << 14, chance)
    priority = chance * count + jnp.arange(count)
    return lax.top_k(priority.astype(jnp.int32), top)[1].astype(jnp.int32)


def split_up(count, total, most, skew):
    loads = [(1 << 20) // math.isqrt(standing ** skew) + 1 for standing in range(2, count + 1)]
    surplus, holding = total - most - (count - 1), [1] * (count - 1)
    while surplus > 0:
        free = [i for i in range(count - 1) if holding[i] < most]
        pool, left = sum([loads[i] for i in free]), surplus
        for i in free:
            more = min(most - holding[i], max(1, left * loads[i] // pool), surplus)
            holding[i] = holding[i] + more
            surplus = surplus - more
    return np.array([most] + holding)


def uneven_parts(stream_key, count, total, reach, skew):
    if count == 2:
        one = jax.random.randint(stream_key, (), max(1, total - reach), min(reach, total - 1) + 1)
        return jnp.stack([one, total - one])
    sizes = jnp.asarray(split_up(count, total, reach, skew), jnp.int32)
    pairs = (count - 1) // 2
    donor, receiver = sizes[1:1 + 2 * pairs:2], sizes[2:2 + 2 * pairs:2]
    room = jnp.minimum(donor - 1, reach - receiver)
    moved = jax.random.randint(jax.random.fold_in(stream_key, 1), (pairs,), 0, 1 << 20) % (room + 1)
    sizes = sizes.at[1:1 + 2 * pairs:2].set(donor - moved).at[2:2 + 2 * pairs:2].set(receiver + moved)
    return sizes[jax.random.permutation(jax.random.fold_in(stream_key, 2), count)]


def gaussian(stream_key, dims, width, reach, cuts=(), kind=jnp.bfloat16):
    result = jax.random.normal(stream_key, dims, jnp.float32) * width
    if len(cuts) > 0:
        result = level_of(stream_key, dims, cuts, -0.22, 0.18) * result
    return jnp.clip(result, min=-reach, max=reach).astype(kind)


def setup_inputs(seed: int = 0) -> dict:
    streams_of = jax.random.split(jax.random.key(seed), 10)
    tokens = gaussian(streams_of[0], (TOKENS, D), 1.0, 6.0, ((0, 1024),))
    routes = picks_of(streams_of[1], TOKENS, EXPERTS, 1, 1024)
    pool_ids = jax.vmap(lambda own: jnp.searchsorted(jnp.cumsum(uneven_parts(own, CLIPS_G, GROUP_TOK, CLIP_MOST, 1)), jnp.arange(GROUP_TOK), side="right"))(jax.random.split(streams_of[2], N_DP)).reshape((N_DP, GROUP_TOK)).astype(jnp.int32)
    w_router = gaussian(streams_of[3], (D, EXPERTS), D ** -0.5, 0.15625)
    w_up = gaussian(streams_of[4], (D, EXPERTS * FFW), D ** -0.5, 0.15625, ((1, 32),))
    w_down = gaussian(streams_of[5], (EXPERTS * FFW, D), FFW ** -0.5, 0.125, ((0, 32),))
    captions = gaussian(streams_of[6], (CAPS, D), 1.0, 6.0, ((0, 32),))
    clip_pairs = jax.random.permutation(streams_of[7], CAPS).astype(jnp.int32)
    teacher = gaussian(streams_of[8], (CAPS, CAPS), 3.0, 12.0, ((0, 32),), jnp.float32)
    return {"tokens": tokens, "routes": routes, "pool_ids": pool_ids, "w_router": w_router, "w_up": w_up, "w_down": w_down, "captions": captions, "clip_pairs": clip_pairs, "teacher": teacher}


HIGHEST = lax.Precision.HIGHEST
logit_scale = 10.0
logit_shift = -10.0
norm_eps = 1e-06

def gelu_back(preact, upstream):
    return jax.vjp(jax.nn.gelu, preact)[1](upstream)[0]

def routing(group_x, group_route, w_router):
    expert_ids = jnp.arange(EXPERTS, dtype=jnp.int32)
    chosen = group_route[:, None] == expert_ids[None, :]
    scores = jnp.dot(group_x, w_router, preferred_element_type=jnp.float32)
    sigmoid_gate = jax.nn.sigmoid(lax.optimization_barrier(jnp.sum(jnp.where(chosen, scores, jnp.zeros_like(scores)), axis=1)))
    blocks = chosen.astype(jnp.int32).reshape(N_EXPERT, TOK_DEV, EXPERTS)
    earlier = (jnp.cumsum(blocks, axis=1) - blocks).reshape(GROUP_TOK, EXPERTS)
    arrival = lax.optimization_barrier(jnp.sum(earlier * chosen.astype(jnp.int32), axis=1))
    source = jnp.arange(GROUP_TOK, dtype=jnp.int32) // TOK_DEV
    total_slots = EXPERTS * N_EXPERT * SLOT
    target = jnp.where(arrival < SLOT, (group_route * N_EXPERT + source) * SLOT + arrival, total_slots)
    table = jnp.full((total_slots,), GROUP_TOK, jnp.int32).at[target].set(jnp.arange(GROUP_TOK, dtype=jnp.int32), mode='drop')
    return (chosen, sigmoid_gate, table)

def padded(values, table):
    extra = jnp.zeros((1,) + values.shape[1:], values.dtype)
    return jnp.concatenate([values, extra], axis=0)[table]

def expert_pass(w_up, w_down, expert, slot_x):
    w_first = lax.dynamic_slice_in_dim(w_up, expert * FFW, FFW, 1)
    w_second = lax.dynamic_slice_in_dim(w_down, expert * FFW, FFW, 0)
    preact = jnp.dot(slot_x, w_first, preferred_element_type=jnp.float32)
    hidden = jax.nn.gelu(preact).astype(jnp.bfloat16)
    produced = jnp.dot(hidden, w_second, preferred_element_type=jnp.float32)
    return (preact, produced, w_first, w_second)

def reference(tokens, routes, pool_ids, w_router, w_up, w_down, captions, clip_pairs, teacher):
    group_x = tokens.reshape(N_DP, GROUP_TOK, D)
    group_route = routes.reshape(N_DP, GROUP_TOK)
    expert_list = jnp.arange(EXPERTS, dtype=jnp.int32)

    def group_pool(inputs):
        local_x, local_route, local_clip = inputs
        chosen, sigmoid_gate, table = routing(local_x, local_route, w_router)
        gating = sigmoid_gate.astype(jnp.bfloat16)
        slot_x = padded(local_x, table).reshape(EXPERTS, N_EXPERT * SLOT, D)

        def forward(pair):
            return expert_pass(w_up, w_down, pair[0], pair[1])[1]
        outputs = lax.map(forward, (expert_list, slot_x))
        expert_tok = jnp.zeros((GROUP_TOK + 1, D), jnp.float32).at[table].set(outputs.reshape(-1, D))[:GROUP_TOK]
        layer_out = local_x.astype(jnp.float32) + gating.astype(jnp.float32)[:, None] * expert_tok
        members = (local_clip[:, None] == jnp.arange(CLIPS_G, dtype=jnp.int32)[None, :]).astype(jnp.float32)
        return (jnp.dot(members.T, layer_out, precision=HIGHEST), lax.optimization_barrier(jnp.sum(members, axis=0)))
    pooled, counts = lax.map(group_pool, (group_x, group_route, pool_ids))
    counts_flat = counts.reshape(CAPS)
    clip_mean = pooled.reshape(CAPS, D) / counts_flat[:, None]
    img_scale = lax.rsqrt(lax.optimization_barrier(jnp.sum(clip_mean * clip_mean, axis=1, keepdims=True)) + norm_eps)
    image_emb = clip_mean * img_scale
    text_raw = captions.astype(jnp.float32)
    text_scale = lax.rsqrt(lax.optimization_barrier(jnp.sum(text_raw * text_raw, axis=1, keepdims=True)) + norm_eps)
    text_emb = text_raw * text_scale
    logits = logit_scale * jnp.dot(image_emb, text_emb.T, precision=HIGHEST) + logit_shift
    matched = (clip_pairs[None, :] == jnp.arange(CAPS, dtype=jnp.int32)[:, None]).astype(jnp.float32)
    target = 0.5 * matched + 0.5 * jax.nn.sigmoid(teacher)
    loss_grad = (jax.nn.sigmoid(logits) - target) * (counts_flat[:, None] / CAPS)
    d_image = logit_scale * jnp.dot(loss_grad, text_emb, precision=HIGHEST)
    d_text = logit_scale * jnp.dot(loss_grad.T, image_emb, precision=HIGHEST)
    caption_grads = text_scale * d_text - text_scale ** 3 * lax.optimization_barrier(jnp.sum(text_raw * d_text, axis=1, keepdims=True)) * text_raw
    mean_grad = img_scale * d_image - img_scale ** 3 * lax.optimization_barrier(jnp.sum(clip_mean * d_image, axis=1, keepdims=True)) * clip_mean
    clip_grad = (mean_grad / counts_flat[:, None]).reshape(N_DP, CLIPS_G, D)

    def group_back(inputs):
        local_x, local_route, local_clip, local_grad = inputs
        chosen, sigmoid_gate, table = routing(local_x, local_route, w_router)
        gating = sigmoid_gate.astype(jnp.bfloat16)
        members = (local_clip[:, None] == jnp.arange(CLIPS_G, dtype=jnp.int32)[None, :]).astype(jnp.float32)
        token_dy = jnp.dot(members, local_grad, precision=HIGHEST)
        slot_x = padded(local_x, table).reshape(EXPERTS, N_EXPERT * SLOT, D)
        slot_dy = padded(token_dy, table).reshape(EXPERTS, N_EXPERT * SLOT, D)
        slot_gate = padded(gating, table).reshape(EXPERTS, N_EXPERT * SLOT)

        def backward(group):
            expert, inputs_x, inputs_dy, inputs_gate = group
            preact, produced, w_first, w_second = expert_pass(w_up, w_down, expert, inputs_x)
            cotangent = (inputs_gate.astype(jnp.float32)[:, None] * inputs_dy).astype(jnp.bfloat16)
            d_hidden = jnp.dot(cotangent, w_second.T, preferred_element_type=jnp.float32)
            d_preact = gelu_back(preact, d_hidden).astype(jnp.bfloat16)
            return (jnp.dot(d_preact, w_first.T, preferred_element_type=jnp.float32), lax.optimization_barrier(jnp.sum(inputs_dy * produced, axis=1)))
        slot_dx, slot_dg = lax.map(backward, (expert_list, slot_x, slot_dy, slot_gate))
        token_dx = jnp.zeros((GROUP_TOK + 1, D), jnp.float32).at[table].set(slot_dx.reshape(-1, D))[:GROUP_TOK]
        token_dg = jnp.zeros((GROUP_TOK + 1,), jnp.float32).at[table].set(slot_dg.reshape(-1))[:GROUP_TOK]
        router_cols = jnp.dot(chosen.astype(jnp.float32), w_router.astype(jnp.float32).T, precision=HIGHEST)
        slope = token_dg * sigmoid_gate * (1.0 - sigmoid_gate)
        return token_dy + token_dx + slope[:, None] * router_cols
    token_grads = lax.map(group_back, (group_x, group_route, pool_ids, clip_grad)).reshape(TOKENS, D)
    return (token_grads, caption_grads)
```

```python
import jax
import jax.numpy as jnp
from jax import lax
from jax.sharding import PartitionSpec as P

HIGHEST = lax.Precision.HIGHEST
logit_scale = 10.0
logit_shift = -10.0
norm_eps = 1e-06
f32 = jnp.float32
bf16 = jnp.bfloat16
LANES = 128


def gelu_back(preact, upstream):
    return jax.vjp(jax.nn.gelu, preact)[1](upstream)[0]


def exchange(x, axis):
    return lax.all_to_all(x, axis, split_axis=0, concat_axis=0, tiled=True)


def shards(tokens, routes, pool_ids, w_router, w_up, w_down, captions, clip_pairs, teacher):
    tok_rows, width = tokens.shape
    n_experts = w_router.shape[1]
    n_clips, n_caps = teacher.shape
    n_dp = lax.axis_size("dp")
    n_exp = lax.axis_size("expert")
    capacity = tok_rows // n_experts
    slot_count = n_experts * capacity
    half = width // 2
    strip = width // n_exp
    own = lax.axis_index("expert")
    core = own % 2
    expert = own // 2
    swap = [(i, i ^ 1) for i in range(n_exp)]

    gathered = exchange(
        jnp.broadcast_to(captions[None], (n_dp,) + captions.shape), "dp"
    ).reshape(n_caps, width)

    route_ids = routes[:, 0]
    chosen = (route_ids[:, None] == jnp.arange(n_experts, dtype=jnp.int32)[None, :]).astype(bf16)
    positions = jnp.arange(tok_rows, dtype=jnp.int32)
    earlier = (positions[:, None] > positions[None, :]).astype(bf16)
    arrival = jnp.sum(
        jnp.dot(earlier, chosen, preferred_element_type=f32) * chosen.astype(f32), axis=1
    )
    slot_index = route_ids.astype(f32) * capacity + arrival
    slot_range = jnp.arange(slot_count, dtype=f32)
    placed = (
        (slot_index[:, None] == slot_range[None, :]) & (arrival < capacity)[:, None]
    ).astype(bf16)
    members = (pool_ids[0][:, None] == jnp.arange(n_clips, dtype=jnp.int32)[None, :]).astype(bf16)
    placed_t = placed.T
    slot_rows = jnp.dot(placed_t, tokens, preferred_element_type=f32).astype(bf16)
    slot_clips = jnp.dot(placed_t, members, preferred_element_type=f32).astype(bf16)
    counts_part = jnp.sum(members.astype(f32), axis=0)
    side = jnp.concatenate(
        [
            slot_clips,
            jnp.broadcast_to(counts_part[None].astype(bf16), (slot_count, n_clips)),
            jnp.zeros((slot_count, LANES - 2 * n_clips), bf16),
        ],
        axis=1,
    ).reshape(n_experts, 1, capacity, LANES)
    halves = slot_rows.reshape(n_experts, capacity, 2, half).transpose(0, 2, 1, 3)
    send = jnp.concatenate(
        [halves, jnp.broadcast_to(side, (n_experts, 2, capacity, LANES))], axis=3
    ).reshape(n_exp, capacity, half + LANES)
    recv = exchange(send, "expert")
    rows_own = recv[..., :half].reshape(n_exp * capacity, half)
    rows_other = lax.ppermute(rows_own, "expert", swap)
    rows = jnp.where(
        core == 0,
        jnp.concatenate([rows_own, rows_other], axis=1),
        jnp.concatenate([rows_other, rows_own], axis=1),
    )
    clip_weights = recv[..., half : half + n_clips].reshape(-1, n_clips).astype(f32)
    counts = jnp.sum(recv[:, 0, half + n_clips : half + 2 * n_clips].astype(f32), axis=0)

    own_col = (jnp.arange(n_experts) == expert).astype(f32)
    scores = jnp.dot(rows, w_router, preferred_element_type=f32)
    sigmoid_gate = jax.nn.sigmoid(jnp.sum(scores * own_col[None], axis=1))
    gate = sigmoid_gate.astype(bf16).astype(f32)
    router_col = jnp.sum(w_router.astype(f32) * own_col[None], axis=1)

    preact = jnp.dot(rows, w_up, preferred_element_type=f32)
    hidden = jax.nn.gelu(preact).astype(bf16)
    produced = jnp.dot(hidden, w_down, preferred_element_type=f32)
    pooled_part = jnp.dot(members.T, tokens, preferred_element_type=f32)
    pooled_part = pooled_part + jnp.dot(
        (clip_weights * gate[:, None]).T, produced, precision=HIGHEST
    )
    quarter = n_clips * width // n_exp
    blocks = width // quarter
    pieces = pooled_part.reshape(n_clips, blocks, quarter).transpose(1, 0, 2)
    pieces = exchange(pieces.reshape(n_exp, 1, quarter), "expert")
    piece = jnp.sum(pieces, axis=0, keepdims=True)
    pooled = exchange(jnp.broadcast_to(piece, (n_exp, 1, quarter)), "expert")
    pooled = pooled.reshape(blocks, n_clips, quarter).transpose(1, 0, 2).reshape(n_clips, width)

    clip_mean = pooled / counts[:, None]
    img_scale = lax.rsqrt(jnp.sum(clip_mean * clip_mean, axis=1, keepdims=True) + norm_eps)
    image_emb = clip_mean * img_scale
    text_raw = gathered.astype(f32)
    text_scale = lax.rsqrt(jnp.sum(text_raw * text_raw, axis=1) + norm_eps)
    raw_dots = jnp.dot(image_emb, text_raw.T, precision=HIGHEST)
    logits = logit_scale * raw_dots * text_scale[None] + logit_shift
    own_clips = lax.axis_index("dp") * n_clips + jnp.arange(n_clips, dtype=jnp.int32)
    matched = (clip_pairs[None, :] == own_clips[:, None]).astype(f32)
    target = 0.5 * matched + 0.5 * jax.nn.sigmoid(teacher)
    loss_grad = (jax.nn.sigmoid(logits) - target) * (counts[:, None] / n_caps)
    d_image = logit_scale * jnp.dot(loss_grad * text_scale[None], text_raw, precision=HIGHEST)
    mean_grad = (
        img_scale * d_image
        - img_scale**3 * jnp.sum(clip_mean * d_image, axis=1, keepdims=True) * clip_mean
    )
    clip_grad = mean_grad / counts[:, None]

    emb_strip = lax.dynamic_slice_in_dim(image_emb, own * strip, strip, 1)
    raw_strip = lax.dynamic_slice_in_dim(gathered, own * strip, strip, 1).astype(f32)
    text_strip = logit_scale * jnp.dot(loss_grad.T, emb_strip, precision=HIGHEST)
    text_dot = logit_scale * jnp.sum(loss_grad * raw_dots, axis=0)
    terms = (
        text_scale[:, None] * text_strip
        - (text_scale**3 * text_dot)[:, None] * raw_strip
    )
    caps_dp = n_caps // n_dp
    strip_grads = jnp.sum(
        exchange(terms.reshape(n_dp, 1, caps_dp * strip), "dp"), axis=(0, 1)
    ).reshape(caps_dp, strip)

    unit_dy = jnp.dot(clip_weights, clip_grad, precision=HIGHEST)
    cotangent = (gate[:, None] * unit_dy).astype(bf16)
    d_hidden = lax.dot_general(
        cotangent, w_down, (((1,), (1,)), ((), ())), preferred_element_type=f32
    )
    d_preact = gelu_back(preact, d_hidden).astype(bf16)
    slope = jnp.sum(unit_dy * produced, axis=1) * sigmoid_gate * (1.0 - sigmoid_gate)

    def part_dx(which):
        w_half = lax.dynamic_slice_in_dim(w_up, which * half, half, 0)
        col = lax.dynamic_slice_in_dim(router_col, which * half, half, 0)
        return (
            lax.dot_general(
                d_preact, w_half, (((1,), (1,)), ((), ())), preferred_element_type=f32
            )
            + slope[:, None] * col[None]
        )

    from_other = lax.ppermute(part_dx(1 - core), "expert", swap)
    dx_half = (part_dx(core) + from_other).astype(bf16).reshape(n_exp, capacity, half)

    high = strip_grads.astype(bf16)
    low = (strip_grads - high.astype(f32)).astype(bf16)
    strips = jnp.concatenate([high, low, jnp.zeros((caps_dp, LANES - 2 * strip), bf16)], axis=1)
    back = exchange(
        jnp.concatenate(
            [dx_half, jnp.broadcast_to(strips[None], (n_exp, caps_dp, LANES))], axis=2
        ),
        "expert",
    )
    slot_dx = (
        back[..., :half]
        .reshape(n_experts, 2, capacity, half)
        .transpose(0, 2, 1, 3)
        .reshape(slot_count, width)
    )
    token_dx = jnp.dot(placed, slot_dx, preferred_element_type=f32)
    token_dy = jnp.dot(members.astype(f32), clip_grad, precision=HIGHEST)
    sides = back[..., half : half + 2 * strip].astype(f32)
    caption_grads = (
        (sides[..., :strip] + sides[..., strip:]).transpose(1, 0, 2).reshape(caps_dp, width)
    )
    return (token_dy + token_dx, caption_grads)


def solution(mesh):
    return jax.shard_map(
        shards,
        mesh=mesh,
        in_specs=(
            P(("dp", "expert"), None),
            P(("dp", "expert"), None),
            P("dp", "expert"),
            P(),
            P(None, "expert"),
            P("expert", None),
            P("dp", None),
            P(),
            P("dp", None),
        ),
        out_specs=(P(("dp", "expert"), None), P("dp", None)),
        check_vma=False,
    )
```

```python
import functools
import jax
import jax.numpy as jnp
from jax import lax
from jax.experimental import pallas as pl
from jax.experimental.pallas import tpu as pltpu
from jax.sharding import PartitionSpec as P

HIGHEST = lax.Precision.HIGHEST
logit_scale = 10.0
logit_shift = -10.0
norm_eps = 1e-06
f32 = jnp.float32
bf16 = jnp.bfloat16
LANES = 128
LOW = 256
MIB = 1 << 20


def exchange(x, axis):
    return lax.all_to_all(x, axis, split_axis=0, concat_axis=0, tiled=True)


def iota(shape, axis):
    return lax.broadcasted_iota(jnp.int32, shape, axis)


def nn(a, b):
    return lax.dot_general(a, b, (((1,), (0,)), ((), ())), preferred_element_type=f32)


def nt(a, b):
    return lax.dot_general(a, b, (((1,), (1,)), ((), ())), preferred_element_type=f32)


def stack3(x):
    high = x.astype(bf16).astype(f32)
    rest = x - high
    mid = rest.astype(bf16).astype(f32)
    return jnp.concatenate([high, mid, rest - mid], axis=0).astype(bf16)


def fold3(x):
    rows = x.shape[0] // 3
    return x[:rows] + (x[rows : 2 * rows] + x[2 * rows :])


def slot_matrix(route_row, capacity, n_experts):
    toks = route_row.shape[1]
    chosen = (iota((n_experts, toks), 0) == route_row).astype(f32)
    earlier = (iota((toks, toks), 0) < iota((toks, toks), 1)).astype(f32).astype(bf16)
    before = nn(chosen.astype(bf16), earlier)
    arrival = jnp.sum(before * chosen, axis=0, keepdims=True)
    slot = route_row.astype(f32) * capacity + arrival
    slot = jnp.where(arrival < capacity, slot, -1.0)
    return (iota((n_experts * capacity, toks), 0).astype(f32) == slot).astype(f32)


def pack_kernel(capacity, n_experts, n_clips, tok_ref, route_ref, pool_ref, send_ref, base_ref, placed_ref):
    toks, width = tok_ref.shape
    half = width // 2
    placed_t = slot_matrix(route_ref[...], capacity, n_experts)
    placed_ref[...] = placed_t.T.astype(bf16)
    placed_t = placed_t.astype(bf16)
    pool = pool_ref[...]
    ids = iota((LANES, toks), 0)
    members = (ids == pool).astype(f32)
    counted = (ids - n_clips == pool).astype(f32).astype(bf16)
    side = nt(placed_t, members.astype(bf16)) + nt(
        jnp.ones((n_experts * capacity, toks), bf16), counted
    )
    side = side.reshape(n_experts, capacity, LANES).astype(bf16)
    tokens = tok_ref[...]
    base_ref[...] = nn(members[:n_clips].astype(bf16), tokens)
    rows = nn(placed_t, tokens)
    for h in range(2):
        send_ref[:, h, :, :half] = (
            rows[:, h * half : (h + 1) * half].reshape(n_experts, capacity, half).astype(bf16)
        )
        send_ref[:, h, :, half:] = side


def forward_kernel(
    n_clips, at_ref, recv_ref, other_ref, router_ref, up_ref, down_ref, base_ref,
    slope_ref, hidden_ref, aux_ref, counts_ref, pooled_ref,
):
    n_exp, capacity, wide = recv_ref.shape
    half = wide - LANES
    rows = n_exp * capacity
    n_experts = router_ref.shape[0]
    expert = at_ref[0]
    own_at = pl.multiple_of(at_ref[1] * half, LANES)
    other_at = pl.multiple_of((1 - at_ref[1]) * half, LANES)
    own = recv_ref[:, :, :half].astype(f32).reshape(rows, half).astype(bf16)
    other = other_ref[:, :, :half].astype(f32).reshape(rows, half).astype(bf16)
    side = recv_ref[:, :, half:].astype(f32).reshape(rows, LANES)
    scores = nt(own, router_ref[:, pl.ds(own_at, half)]) + nt(
        other, router_ref[:, pl.ds(other_at, half)]
    )
    mine = iota((rows, n_experts), 1) == expert
    score = jnp.sum(jnp.where(mine, scores, 0.0), axis=1, keepdims=True)
    sigmoid_gate = jax.nn.sigmoid(score)
    gate = sigmoid_gate.astype(bf16).astype(f32)
    lane = iota((rows, LANES), 1)
    clip = jnp.where(lane < n_clips, side, 0.0)
    aux_ref[...] = jnp.where(
        lane == n_clips,
        gate,
        jnp.where(lane == n_clips + 1, sigmoid_gate * (1.0 - sigmoid_gate), clip),
    )
    preact = nn(own, up_ref[pl.ds(own_at, half), :]) + nn(other, up_ref[pl.ds(other_at, half), :])
    root = 0.7978845608028654
    square = preact * preact
    tanh = jnp.tanh(root * (preact + 0.044715 * (square * preact)))
    hidden = (preact * (0.5 * (1.0 + tanh))).astype(bf16)
    hidden_ref[...] = hidden
    slope_ref[...] = 0.5 * (1.0 + tanh) + 0.5 * preact * (1.0 - tanh * tanh) * (
        root * (1.0 + (3 * 0.044715) * square)
    )
    produced = nn(hidden, down_ref[...])
    side_t = side.T
    counts_ref[...] = jnp.broadcast_to(
        jnp.sum(side_t[n_clips : 2 * n_clips], axis=1, keepdims=True) / capacity,
        (n_clips, LANES),
    )
    weights = (clip * gate).T[:n_clips].astype(bf16)
    high = produced.astype(bf16)
    low = (produced - high.astype(f32)).astype(bf16)
    pooled_ref[...] = base_ref[...] + (nn(weights, high) + nn(weights, low))


def loss_kernel(
    caps_dp, at_ref, pooled_ref, counts_ref, own_text_ref, other_text_ref, pairs_ref, teacher_ref,
    strip_ref, grad_ref, terms_ref, mean_ref, image_ref, d_image_ref,
):
    n_clips, width = pooled_ref.shape
    n_caps = teacher_ref.shape[1]
    half = width // 2
    own_at = pl.multiple_of(at_ref[1] * half, LANES)
    other_at = pl.multiple_of((1 - at_ref[1]) * half, LANES)
    own_dp = at_ref[2]
    counts = counts_ref[:, :1]
    clip_mean = pooled_ref[...] / counts
    img_scale = lax.rsqrt(jnp.sum(clip_mean * clip_mean, axis=1, keepdims=True) + norm_eps)
    image_emb = clip_mean * img_scale
    mean_ref[...] = clip_mean
    image_ref[...] = image_emb
    own_text = own_text_ref[...]
    other_text = other_text_ref[...]
    ones = jnp.ones((16, half), bf16)

    def squares(text):
        square = text.astype(f32) * text.astype(f32)
        high = square.astype(bf16)
        return nt(ones, high) + nt(ones, (square - high.astype(f32)).astype(bf16))

    text_scale = lax.rsqrt((squares(own_text) + squares(other_text))[:n_clips] + norm_eps)
    raw = fold3(
        nt(stack3(image_ref[:, pl.ds(own_at, half)]), own_text)
        + nt(stack3(image_ref[:, pl.ds(other_at, half)]), other_text)
    )
    order = (
        iota((n_caps, n_caps), 0) == (iota((n_caps, n_caps), 1) ^ (own_dp * caps_dp))
    ).astype(f32).astype(bf16)
    matched = (pairs_ref[...] == own_dp * n_clips + iota((n_clips, n_caps), 0)).astype(f32)
    target = fold3(nn(stack3(0.5 * matched + 0.5 * jax.nn.sigmoid(teacher_ref[...])), order))
    logits = logit_scale * raw * text_scale + logit_shift
    loss_grad = (jax.nn.sigmoid(logits) - target) * (counts / n_caps)
    scaled = loss_grad * text_scale
    scaled3 = stack3(scaled)
    d_image_ref[:, pl.ds(own_at, half)] = logit_scale * fold3(nn(scaled3, own_text))
    d_image_ref[:, pl.ds(other_at, half)] = logit_scale * fold3(nn(scaled3, other_text))
    d_image = d_image_ref[...]
    mean_grad = (
        img_scale * d_image
        - img_scale
        * img_scale
        * img_scale
        * jnp.sum(clip_mean * d_image, axis=1, keepdims=True)
        * clip_mean
    )
    grad_ref[...] = mean_grad / counts
    pick = strip_ref[...]
    emb_strip = fold3(nn(stack3(image_emb), pick))
    own_strip = strip_ref.at[pl.ds(own_at, half), :][...]
    other_strip = strip_ref.at[pl.ds(other_at, half), :][...]
    raw_strip = nn(own_text, own_strip) + nn(other_text, other_strip)
    dots = jnp.sum(loss_grad * raw, axis=0, keepdims=True)
    cube = text_scale[:1] * text_scale[:1] * text_scale[:1] * dots
    both = jnp.concatenate([scaled, jnp.broadcast_to(cube, scaled.shape)], axis=0)
    both = jnp.concatenate([both, jnp.zeros((LANES - both.shape[0], n_caps), f32)], axis=0).T
    left = both[:, :n_clips]
    products = lax.dot_general(
        left, emb_strip, (((1,), (0,)), ((), ())), precision=HIGHEST, preferred_element_type=f32
    )
    terms = logit_scale * (products - both[:, n_clips : n_clips + 1] * raw_strip)
    high = terms.astype(bf16)
    rest = terms - high.astype(f32)
    mid = rest.astype(bf16)
    low = (rest - mid.astype(f32)).astype(bf16)
    terms = nn(order, high) + (nn(order, mid) + nn(order, low))
    terms_ref[...] = terms.reshape(terms_ref.shape)


def backward_kernel(
    n_clips, at_ref, grad_ref, aux_ref, slope_ref, hidden_ref, down_ref, up_ref, router_ref,
    d_preact_ref, out_ref, part_ref, stacked_ref,
):
    rows, hid = hidden_ref.shape
    width = grad_ref.shape[1]
    half = width // 2
    expert = at_ref[0]
    other_at = pl.multiple_of((1 - at_ref[1]) * half, LANES)
    aux = aux_ref[...]
    lane = iota((rows, LANES), 1)
    clip = jnp.sum(jnp.where(lane < n_clips, aux * lane.astype(f32), 0.0), axis=1, keepdims=True)
    gate = aux[:, n_clips : n_clips + 1]
    gate_slope = aux[:, n_clips + 1 : n_clips + 2]
    lane3 = lane % n_clips
    thrice = ((lane3.astype(f32) == clip) & (lane < 3 * n_clips)).astype(f32).astype(bf16)
    grads = grad_ref[...]
    high = grads.astype(bf16).astype(f32)
    rest = grads - high
    mid = rest.astype(bf16).astype(f32)
    parts = jnp.concatenate(
        [high, mid, rest - mid, jnp.zeros((LANES - 3 * n_clips, width), f32)], axis=0
    ).astype(bf16)
    unit_dy = nn(thrice, parts)
    stacked_ref[:rows, :] = (gate * unit_dy).astype(bf16)
    stacked_ref[rows:, :] = jnp.concatenate([high, mid], axis=0).astype(bf16)
    d_all = nt(stacked_ref[...], down_ref[...])
    d_preact = (d_all[:rows] * slope_ref[...]).astype(bf16)
    d_preact_ref[...] = d_preact
    by_clip = d_all[rows : rows + n_clips] + d_all[rows + n_clips :]
    high_v = by_clip.astype(bf16).astype(f32)
    two = jnp.concatenate([high_v, by_clip - high_v], axis=0).astype(bf16)
    dots = nt(hidden_ref[...], two)
    lane2 = iota((rows, 2 * n_clips), 1) % n_clips
    token_dg = jnp.sum(
        jnp.where(lane2.astype(f32) == clip, dots, 0.0), axis=1, keepdims=True
    )
    part = token_dg * gate_slope
    part_ref[...] = jnp.broadcast_to(part, (rows, LANES))
    router = jnp.sum(
        jnp.where(
            iota((router_ref.shape[0], half), 0) == expert,
            router_ref[:, pl.ds(other_at, half)].astype(f32),
            0.0,
        ),
        axis=0,
        keepdims=True,
    )
    out_ref[...] = nt(d_preact, up_ref[pl.ds(other_at, half), :]) + part * router


def own_kernel(at_ref, d_preact_ref, part_ref, up_ref, router_ref, out_ref):
    half = out_ref.shape[1]
    expert = at_ref[0]
    own_at = pl.multiple_of(at_ref[1] * half, LANES)
    router = jnp.sum(
        jnp.where(
            iota((router_ref.shape[0], half), 0) == expert,
            router_ref[:, pl.ds(own_at, half)].astype(f32),
            0.0,
        ),
        axis=0,
        keepdims=True,
    )
    out_ref[...] = nt(d_preact_ref[...], up_ref[pl.ds(own_at, half), :]) + part_ref[:, :1] * router


def return_kernel(own_ref, other_ref, terms_ref, pay_ref):
    n_exp, capacity, _ = pay_ref.shape
    half = own_ref.shape[1]
    total = (own_ref[...] + other_ref[...]).reshape(n_exp, capacity, half)
    high = total.astype(bf16)
    pay_ref[:, :, :half] = high
    pay_ref[:, :, half : half + LOW] = (
        total[:, :, :LOW] - high[:, :, :LOW].astype(f32)
    ).astype(bf16)
    strip = jnp.sum(terms_ref[...], axis=0)
    strip_high = strip.astype(bf16).astype(f32)
    side = strip_high + pltpu.roll(strip - strip_high, LANES // 2, 1)
    pay_ref[:, :, half + LOW :] = jnp.broadcast_to(
        side.astype(bf16)[None], (n_exp, capacity, LANES)
    )


def final_kernel(strip, back_ref, placed_ref, dy_ref, out_ref, caps_ref):
    n_experts, _, capacity, wide = back_ref.shape
    half = wide - LOW - LANES
    placed = placed_ref[...]
    slots = n_experts * capacity

    def pick(h, start, size):
        part = back_ref[:, h, :, start : start + size]
        return nn(placed, part.astype(f32).reshape(slots, size).astype(bf16))

    for h in range(2):
        at = h * half
        high = pick(h, 0, half)
        out_ref[:, at : at + LOW] = dy_ref[:, at : at + LOW] + (
            high[:, :LOW] + pick(h, half, LOW)
        )
        out_ref[:, at + LOW : at + half] = dy_ref[:, at + LOW : at + half] + high[:, LOW:]
    lane = iota((capacity, LANES), 1)
    tiles = [jnp.zeros((capacity, LANES), f32) for _ in range(caps_ref.shape[1] // LANES)]
    for e in range(2 * n_experts):
        side = back_ref[e // 2, e % 2, :, half + LOW :].astype(f32)
        value = jnp.where(lane < strip, side + pltpu.roll(side, LANES // 2, 1), 0.0)
        tile, offset = divmod(e * strip, LANES)
        if offset:
            value = pltpu.roll(value, offset, 1)
        tiles[tile] = tiles[tile] + jnp.where(lane >= offset, value, 0.0)
        if offset + strip > LANES:
            tiles[tile + 1] = tiles[tile + 1] + jnp.where(lane < offset, value, 0.0)
    for t, value in enumerate(tiles):
        caps_ref[:, t * LANES : (t + 1) * LANES] = value


def shards(tokens, routes, pool_ids, w_router, w_up, w_down, captions, clip_pairs, teacher):
    tok_rows, width = tokens.shape
    n_experts = w_router.shape[1]
    n_clips, n_caps = teacher.shape
    hid = w_up.shape[1]
    n_dp = lax.axis_size("dp")
    n_exp = lax.axis_size("expert")
    caps_dp = n_caps // n_dp
    capacity = tok_rows // n_experts
    half = width // 2
    strip = width // n_exp
    rows = n_exp * capacity
    own = lax.axis_index("expert")
    own_dp = lax.axis_index("dp")
    core = own % 2
    at = jnp.stack([own // 2, core, own_dp]).astype(jnp.int32)
    at_spec = pl.BlockSpec(memory_space=pltpu.SMEM)
    swap = [(i, i ^ 1) for i in range(n_exp)]
    route_row = routes.reshape(1, tok_rows)
    router_t = w_router.T
    sds = jax.ShapeDtypeStruct

    def run(body, outs, operands, scratch=(), flops=0, moved=0):
        vmem = pl.BlockSpec(memory_space=pltpu.VMEM)
        return pl.pallas_call(
            body,
            out_shape=outs,
            in_specs=[at_spec if o is at else vmem for o in operands],
            out_specs=jax.tree.map(lambda _: vmem, outs),
            scratch_shapes=list(scratch),
            compiler_params=pltpu.CompilerParams(vmem_limit_bytes=32 * MIB),
            cost_estimate=pl.CostEstimate(flops=flops, bytes_accessed=moved, transcendentals=0),
        )(*operands)

    def after(x, *others):
        return lax.optimization_barrier((x,) + others)[0]

    def from_dp(x, mask):
        return lax.ppermute(x, "dp", [(i, i ^ mask) for i in range(n_dp)])

    send, base, placed = run(
        functools.partial(pack_kernel, capacity, n_experts, n_clips),
        [
            sds((n_experts, 2, capacity, half + LANES), bf16),
            sds((n_clips, width), f32),
            sds((tok_rows, n_experts * capacity), bf16),
        ],
        [tokens, route_row, pool_ids],
        flops=2 * tok_rows * tok_rows * width,
        moved=3 * tok_rows * width * 2,
    )
    block = after(lax.dynamic_slice_in_dim(captions, core * half, half, 1), send)
    blocks = [block] + [from_dp(block, mask) for mask in range(1, min(4, n_dp))]
    blocks = jnp.concatenate(blocks[: min(4, n_dp)])
    mask = 4
    if mask < n_dp:
        blocks = jnp.concatenate([blocks, from_dp(blocks, mask)])
        mask = 2 * mask

    recv = exchange(send.reshape(n_exp, capacity, half + LANES), "expert")
    other = lax.ppermute(recv, "expert", swap)
    if mask < n_dp:
        blocks = after(blocks, recv)
        blocks = jnp.concatenate([blocks, from_dp(blocks, mask)])
        mask = 2 * mask
    gelu_slope, hidden, aux, counts, pooled_part = run(
        functools.partial(forward_kernel, n_clips),
        [
            sds((rows, hid), f32),
            sds((rows, hid), bf16),
            sds((rows, LANES), f32),
            sds((n_clips, LANES), f32),
            sds((n_clips, width), f32),
        ],
        [at, recv, other, router_t, w_up, w_down, base],
        flops=4 * rows * width * hid,
        moved=4 * width * hid + 6 * rows * hid,
    )
    quarter = n_clips * width // n_exp
    parts = width // quarter
    pieces = pooled_part.reshape(n_clips, parts, quarter).transpose(1, 0, 2)
    pieces = pieces.reshape(n_exp, 1, quarter)
    if mask < n_dp:
        blocks = after(blocks, pieces)
        blocks = jnp.concatenate([blocks, from_dp(blocks, mask)])
        mask = 2 * mask
    piece = jnp.sum(exchange(pieces, "expert"), axis=0, keepdims=True)
    pooled = exchange(jnp.broadcast_to(piece, (n_exp, 1, quarter)), "expert")
    pooled = pooled.reshape(parts, n_clips, quarter).transpose(1, 0, 2).reshape(n_clips, width)
    other_blocks = lax.ppermute(blocks, "expert", swap)

    picks = (
        jnp.arange(width, dtype=jnp.int32)[:, None] - own * strip
        == jnp.arange(LANES, dtype=jnp.int32)[None, :]
    ) & (jnp.arange(LANES) < strip)[None, :]
    clip_grad, terms = run(
        functools.partial(loss_kernel, caps_dp),
        [sds((n_clips, width), f32), sds((n_dp, caps_dp, LANES), f32)],
        [
            at, pooled, counts, blocks, other_blocks, clip_pairs.reshape(1, n_caps), teacher,
            picks.astype(bf16),
        ],
        scratch=[pltpu.VMEM((n_clips, width), f32)] * 3,
        flops=8 * 24 * n_caps * width,
        moved=4 * n_caps * width,
    )
    terms = exchange(terms, "dp")

    d_preact, dx_other, part = run(
        functools.partial(backward_kernel, n_clips),
        [sds((rows, hid), bf16), sds((rows, half), f32), sds((rows, LANES), f32)],
        [at, clip_grad, aux, gelu_slope, hidden, w_down, w_up, router_t],
        scratch=[pltpu.VMEM((rows + 2 * n_clips, width), bf16)],
        flops=3 * rows * width * hid,
        moved=4 * width * hid + 6 * rows * hid,
    )
    from_other = lax.ppermute(dx_other, "expert", swap)
    dx_own = run(
        own_kernel,
        sds((rows, half), f32),
        [at, d_preact, part, w_up, router_t],
        flops=rows * width * hid,
        moved=width * hid + 6 * rows * hid,
    )
    pay = run(
        return_kernel,
        sds((n_exp, capacity, half + LOW + LANES), bf16),
        [dx_own, from_other, terms],
        flops=4 * rows * half,
        moved=12 * rows * half,
    )
    back = exchange(pay, "expert")
    members = (pool_ids[0][:, None] == jnp.arange(n_clips, dtype=jnp.int32)[None, :]).astype(f32)
    token_dy = jnp.dot(members, clip_grad, precision=HIGHEST)
    token_grads, caption_grads = run(
        functools.partial(final_kernel, strip),
        [sds((tok_rows, width), f32), sds((caps_dp, width), f32)],
        [back.reshape(n_experts, 2, capacity, half + LOW + LANES), placed, token_dy],
        flops=4 * tok_rows * tok_rows * width,
        moved=8 * tok_rows * width,
    )
    return (token_grads, caption_grads)


def solution(mesh):
    return jax.shard_map(
        shards,
        mesh=mesh,
        in_specs=(
            P(("dp", "expert"), None),
            P(("dp", "expert"), None),
            P("dp", "expert"),
            P(),
            P(None, "expert"),
            P("expert", None),
            P("dp", None),
            P(),
            P("dp", None),
        ),
        out_specs=(P(("dp", "expert"), None), P("dp", None)),
        check_vma=False,
    )
```

```python
import functools
import jax
import jax.numpy as jnp
from jax import lax
from jax.experimental import pallas as pl
from jax.experimental.pallas import tpu as pltpu
from jax.sharding import PartitionSpec as P

HIGHEST = lax.Precision.HIGHEST
logit_scale = 10.0
logit_shift = -10.0
norm_eps = 1e-06
f32 = jnp.float32
bf16 = jnp.bfloat16
LANES = 128
LOW = 256
MIB = 1 << 20
OWN_FLOPS = 10_000_000_000


def exchange(x, axis):
    return lax.all_to_all(x, axis, split_axis=0, concat_axis=0, tiled=True)


class Late:
    def __init__(self, copy, ref):
        self.copy, self.ref, self.waited = copy, ref, False
        copy.start()

    def ready(self):
        if not self.waited:
            self.copy.wait()
            self.waited = True
        return self.ref


class Leaving:
    def __init__(self, copy, ref):
        self.copy, self.ref, self.sent = copy, ref, False

    def send(self, value):
        self.ref[...] = value
        self.copy.start()
        self.sent = True


def iota(shape, axis):
    return lax.broadcasted_iota(jnp.int32, shape, axis)


def nn(a, b):
    return lax.dot_general(a, b, (((1,), (0,)), ((), ())), preferred_element_type=f32)


def nt(a, b):
    return lax.dot_general(a, b, (((1,), (1,)), ((), ())), preferred_element_type=f32)


def stack3(x):
    high = x.astype(bf16).astype(f32)
    rest = x - high
    mid = rest.astype(bf16).astype(f32)
    return jnp.concatenate([high, mid, rest - mid], axis=0).astype(bf16)


def fold3(x):
    rows = x.shape[0] // 3
    return x[:rows] + (x[rows : 2 * rows] + x[2 * rows :])


def slot_matrix(route_row, capacity, n_experts):
    toks = route_row.shape[1]
    chosen = (iota((n_experts, toks), 0) == route_row).astype(f32)
    earlier = (iota((toks, toks), 0) < iota((toks, toks), 1)).astype(f32).astype(bf16)
    before = nn(chosen.astype(bf16), earlier)
    arrival = jnp.sum(before * chosen, axis=0, keepdims=True)
    slot = route_row.astype(f32) * capacity + arrival
    slot = jnp.where(arrival < capacity, slot, -1.0)
    return (iota((n_experts * capacity, toks), 0).astype(f32) == slot).astype(f32)


def pack_kernel(capacity, n_experts, n_clips, route, pool, tok, send_ref, base_ref, placed_ref):
    toks, width = tok.ref.shape
    half = width // 2
    placed_t = slot_matrix(route.ready()[...], capacity, n_experts)
    placed_ref[...] = placed_t.T.astype(bf16)
    placed_t = placed_t.astype(bf16)
    pool = pool.ready()[...]
    ids = iota((LANES, toks), 0)
    members = (ids == pool).astype(f32)
    counted = (ids - n_clips == pool).astype(f32).astype(bf16)
    side = nt(placed_t, members.astype(bf16)) + nt(
        jnp.ones((n_experts * capacity, toks), bf16), counted
    )
    side = side.reshape(n_experts, capacity, LANES).astype(bf16)
    tokens = tok.ready()[...]
    rows = nn(placed_t, tokens)
    for h in range(2):
        send_ref[:, h, :, :half] = (
            rows[:, h * half : (h + 1) * half].reshape(n_experts, capacity, half).astype(bf16)
        )
        send_ref[:, h, :, half:] = side
    base_ref[...] = nn(members[:n_clips].astype(bf16), tokens)


def cut_strip(tiles, e, strip):
    tile, offset = divmod(e * strip, LANES)
    lane = iota(tiles[0].shape, 1)
    value = tiles[tile]
    if offset + strip > LANES:
        value = jnp.where(lane >= offset, value, tiles[tile + 1])
    if offset:
        value = pltpu.roll(value, LANES - offset, 1)
    return jnp.where(lane < strip, value, 0.0)


def join_strips(strips, strip, n_tiles):
    lane = iota(strips[0].shape, 1)
    tiles = [jnp.zeros(strips[0].shape, f32) for _ in range(n_tiles)]
    for e, value in enumerate(strips):
        tile, offset = divmod(e * strip, LANES)
        if offset:
            value = pltpu.roll(value, offset, 1)
        if offset + strip > LANES:
            tiles[tile] = tiles[tile] + jnp.where(lane >= offset, value, 0.0)
            tiles[tile + 1] = tiles[tile + 1] + jnp.where(lane < offset, value, 0.0)
        else:
            tiles[tile] = tiles[tile] + value
    return tiles


def spread3(value, strip):
    high = value.astype(bf16).astype(f32)
    rest = value - high
    mid = rest.astype(bf16).astype(f32)
    return high + pltpu.roll(mid, strip, 1) + pltpu.roll(rest - mid, 2 * strip, 1)


def gather3(value, strip):
    lane = iota(value.shape, 1)
    low = pltpu.roll(value, LANES - 2 * strip, 1)
    mid = pltpu.roll(value, LANES - strip, 1)
    return jnp.where(lane < strip, value + (mid + low), 0.0)


def forward_kernel(
    n_clips, strip, at_ref, recv, other, router, up, block, down, base, slope, hidden_out, aux_out, counts, pay_ref,
):
    n_exp, capacity, wide = recv.ref.shape
    half = wide - LANES
    rows = n_exp * capacity
    n_experts = router.ref.shape[0]
    expert = at_ref[0]
    own_at = pl.multiple_of(at_ref[1] * half, LANES)
    other_at = pl.multiple_of((1 - at_ref[1]) * half, LANES)
    recv_ref = recv.ready()
    own = recv_ref[:, :, :half].astype(f32).reshape(rows, half).astype(bf16)
    side = recv_ref[:, :, half:].astype(f32).reshape(rows, LANES)
    other_rows = other.ready()[:, :, :half].astype(f32).reshape(rows, half).astype(bf16)
    router_ref = router.ready()
    scores = nt(own, router_ref[:, pl.ds(own_at, half)]) + nt(
        other_rows, router_ref[:, pl.ds(other_at, half)]
    )
    mine = iota((rows, n_experts), 1) == expert
    score = jnp.sum(jnp.where(mine, scores, 0.0), axis=1, keepdims=True)
    sigmoid_gate = jax.nn.sigmoid(score)
    gate = sigmoid_gate.astype(bf16).astype(f32)
    lane = iota((rows, LANES), 1)
    clip = jnp.where(lane < n_clips, side, 0.0)
    aux_out.send(
        jnp.where(
            lane == n_clips,
            gate,
            jnp.where(lane == n_clips + 1, sigmoid_gate * (1.0 - sigmoid_gate), clip),
        )
    )
    side_t = side.T
    counts.send(
        jnp.broadcast_to(
            jnp.sum(side_t[n_clips : 2 * n_clips], axis=1, keepdims=True) / capacity,
            (n_clips, LANES),
        )
    )
    weights = (clip * gate).T[:n_clips].astype(bf16)
    up_ref = up.ready()
    preact = nn(own, up_ref[pl.ds(own_at, half), :]) + nn(
        other_rows, up_ref[pl.ds(other_at, half), :]
    )
    root = 0.7978845608028654
    square = preact * preact
    tanh = jnp.tanh(root * (preact + 0.044715 * (square * preact)))
    hidden = (preact * (0.5 * (1.0 + tanh))).astype(bf16)
    hidden_out.send(hidden)
    slope.send(
        0.5 * (1.0 + tanh)
        + 0.5 * preact * (1.0 - tanh * tanh) * (root * (1.0 + (3 * 0.044715) * square))
    )
    captions = block.ready()
    for h in range(2):
        pay_ref[:, h, :, :half] = jnp.broadcast_to(
            captions[:, h * half : (h + 1) * half][None], (n_exp // 2, captions.shape[0], half)
        )
    produced = nn(hidden, down.ready()[...])
    high = produced.astype(bf16)
    low = (produced - high.astype(f32)).astype(bf16)
    pooled = base.ready()[...] + (nn(weights, high) + nn(weights, low))
    tiles = [pooled[:, t * LANES : (t + 1) * LANES] for t in range(pooled.shape[1] // LANES)]
    for e in range(n_exp):
        pay_ref[e // 2, e % 2, :, half:] = spread3(cut_strip(tiles, e, strip), strip).astype(bf16)


def sum_kernel(strip, side, out_ref):
    total = jnp.sum(side.ready()[...].astype(f32), axis=0)
    total = spread3(gather3(total, strip), strip).astype(bf16)
    out_ref[...] = jnp.broadcast_to(total[None], out_ref.shape)


def loss_kernel(
    strip, at_ref, sums_ref, counts, own, other, pairs, teacher, grad_out, terms_out,
    mean_ref, image_ref, d_image_ref, text_ref,
):
    n_exp, n_clips, wide = own.ref.shape
    n_caps = teacher.ref.shape[1]
    half = wide - LANES
    width = 2 * half
    own_at = pl.multiple_of(at_ref[1] * half, LANES)
    other_at = pl.multiple_of((1 - at_ref[1]) * half, LANES)
    own_dp = at_ref[2]
    n_tiles = width // LANES
    tiles = join_strips(
        [gather3(sums_ref[e].astype(f32), strip) for e in range(n_exp)], strip, n_tiles
    )
    counts = counts.ready()[:, :1]
    for t, tile in enumerate(tiles):
        mean_ref[:, t * LANES : (t + 1) * LANES] = tile / counts
    clip_mean = mean_ref[...]
    img_scale = lax.rsqrt(jnp.sum(clip_mean * clip_mean, axis=1, keepdims=True) + norm_eps)
    image_emb = clip_mean * img_scale
    image_ref[...] = image_emb
    own_text = own.ready()[:, :, :half].astype(f32).reshape(n_caps, half)
    other_text = other.ready()[:, :, :half].astype(f32).reshape(n_caps, half)
    ones = jnp.ones((16, half), bf16)

    def squares(text):
        square = text * text
        high = square.astype(bf16)
        return nt(ones, high) + nt(ones, (square - high.astype(f32)).astype(bf16))

    text_scale = lax.rsqrt((squares(own_text) + squares(other_text))[:n_clips] + norm_eps)
    own_text = own_text.astype(bf16)
    other_text = other_text.astype(bf16)
    text_ref[:, pl.ds(own_at, half)] = own_text
    text_ref[:, pl.ds(other_at, half)] = other_text
    text = text_ref[...]
    raw = fold3(nt(stack3(image_emb), text))
    matched = (
        pairs.ready()[...] == own_dp * n_clips + iota((n_clips, n_caps), 0)
    ).astype(f32)
    target = 0.5 * matched + 0.5 * jax.nn.sigmoid(teacher.ready()[...])
    logits = logit_scale * raw * text_scale + logit_shift
    loss_grad = (jax.nn.sigmoid(logits) - target) * (counts / n_caps)
    scaled = loss_grad * text_scale
    d_image = logit_scale * fold3(nn(stack3(scaled), text))
    mean_grad = (
        img_scale * d_image
        - img_scale
        * img_scale
        * img_scale
        * jnp.sum(clip_mean * d_image, axis=1, keepdims=True)
        * clip_mean
    )
    grad_out.send(mean_grad / counts)
    pick = (
        (iota((width, LANES), 0) - at_ref[3] * strip == iota((width, LANES), 1))
        & (iota((width, LANES), 1) < strip)
    ).astype(f32).astype(bf16)
    emb_strip = fold3(nn(stack3(image_emb), pick))
    raw_strip = nn(text, pick)
    dots = jnp.sum(loss_grad * raw, axis=0, keepdims=True)
    cube = text_scale[:1] * text_scale[:1] * text_scale[:1] * dots
    both = jnp.concatenate([scaled, jnp.broadcast_to(cube, scaled.shape)], axis=0)
    both = jnp.concatenate([both, jnp.zeros((LANES - both.shape[0], n_caps), f32)], axis=0).T
    products = lax.dot_general(
        both[:, :n_clips], emb_strip, (((1,), (0,)), ((), ())),
        precision=HIGHEST, preferred_element_type=f32,
    )
    terms = logit_scale * (products - both[:, n_clips : n_clips + 1] * raw_strip)
    terms_out.send(terms.reshape(terms_out.ref.shape))


def backward_kernel(
    n_clips, at_ref, grad, aux, down, slope, hidden, router, up,
    d_preact_out, out, part_out, stacked_ref,
):
    rows, hid = hidden.ref.shape
    width = grad.ref.shape[1]
    half = width // 2
    expert = at_ref[0]
    other_at = pl.multiple_of((1 - at_ref[1]) * half, LANES)
    grads = grad.ready()[...]
    aux = aux.ready()[...]
    lane = iota((rows, LANES), 1)
    clip = jnp.sum(jnp.where(lane < n_clips, aux * lane.astype(f32), 0.0), axis=1, keepdims=True)
    gate = aux[:, n_clips : n_clips + 1]
    gate_slope = aux[:, n_clips + 1 : n_clips + 2]
    lane3 = lane % n_clips
    thrice = ((lane3.astype(f32) == clip) & (lane < 3 * n_clips)).astype(f32).astype(bf16)
    high = grads.astype(bf16).astype(f32)
    rest = grads - high
    mid = rest.astype(bf16).astype(f32)
    parts = jnp.concatenate(
        [high, mid, rest - mid, jnp.zeros((LANES - 3 * n_clips, width), f32)], axis=0
    ).astype(bf16)
    unit_dy = nn(thrice, parts)
    stacked_ref[:rows, :] = (gate * unit_dy).astype(bf16)
    stacked_ref[rows:, :] = jnp.concatenate([high, mid], axis=0).astype(bf16)
    d_all = nt(stacked_ref[...], down.ready()[...])
    d_preact = (d_all[:rows] * slope.ready()[...]).astype(bf16)
    d_preact_out.send(d_preact)
    by_clip = d_all[rows : rows + n_clips] + d_all[rows + n_clips :]
    high_v = by_clip.astype(bf16).astype(f32)
    two = jnp.concatenate([high_v, by_clip - high_v], axis=0).astype(bf16)
    dots = nt(hidden.ready()[...], two)
    lane2 = iota((rows, 2 * n_clips), 1) % n_clips
    token_dg = jnp.sum(
        jnp.where(lane2.astype(f32) == clip, dots, 0.0), axis=1, keepdims=True
    )
    part = token_dg * gate_slope
    part_out.send(jnp.broadcast_to(part, (rows, LANES)))
    router = jnp.sum(
        jnp.where(
            iota((router.ref.shape[0], half), 0) == expert,
            router.ready()[:, pl.ds(other_at, half)].astype(f32),
            0.0,
        ),
        axis=0,
        keepdims=True,
    )
    out.send(nt(d_preact, up.ready()[pl.ds(other_at, half), :]) + part * router)


def own_kernel(at_ref, d_preact, up, part, router, out):
    half = out.ref.shape[1]
    expert = at_ref[0]
    own_at = pl.multiple_of(at_ref[1] * half, LANES)
    router = jnp.sum(
        jnp.where(
            iota((router.ref.shape[0], half), 0) == expert,
            router.ready()[:, pl.ds(own_at, half)].astype(f32),
            0.0,
        ),
        axis=0,
        keepdims=True,
    )
    out.send(
        nt(d_preact.ready()[...], up.ready()[pl.ds(own_at, half), :])
        + part.ready()[:, :1] * router
    )


def return_kernel(own, other, terms, pay_ref):
    n_exp, capacity, _ = pay_ref.shape
    half = own.ref.shape[1]
    strip = jnp.sum(terms.ready()[...], axis=0)
    strip_high = strip.astype(bf16).astype(f32)
    side = strip_high + pltpu.roll(strip - strip_high, LANES // 2, 1)
    pay_ref[:, :, half + LOW :] = jnp.broadcast_to(
        side.astype(bf16)[None], (n_exp, capacity, LANES)
    )
    total = (own.ready()[...] + other.ready()[...]).reshape(n_exp, capacity, half)
    high = total.astype(bf16)
    pay_ref[:, :, :half] = high
    pay_ref[:, :, half : half + LOW] = (
        total[:, :, :LOW] - high[:, :, :LOW].astype(f32)
    ).astype(bf16)


def final_kernel(strip, back_ref, placed_ref, dy_ref, out_ref, caps_ref):
    n_experts, _, capacity, wide = back_ref.shape
    half = wide - LOW - LANES
    placed = placed_ref[...]
    slots = n_experts * capacity

    def pick(h, start, size):
        part = back_ref[:, h, :, start : start + size]
        return nn(placed, part.astype(f32).reshape(slots, size).astype(bf16))

    for h in range(2):
        at = h * half
        high = pick(h, 0, half)
        out_ref[:, at : at + LOW] = dy_ref[:, at : at + LOW] + (
            high[:, :LOW] + pick(h, half, LOW)
        )
        out_ref[:, at + LOW : at + half] = dy_ref[:, at + LOW : at + half] + high[:, LOW:]
    lane = iota((capacity, LANES), 1)
    strips = []
    for e in range(2 * n_experts):
        side = back_ref[e // 2, e % 2, :, half + LOW :].astype(f32)
        strips.append(jnp.where(lane < strip, side + pltpu.roll(side, LANES // 2, 1), 0.0))
    for t, value in enumerate(join_strips(strips, strip, caps_ref.shape[1] // LANES)):
        caps_ref[:, t * LANES : (t + 1) * LANES] = value


def shards(tokens, routes, pool_ids, w_router, w_up, w_down, captions, clip_pairs, teacher):
    tok_rows, width = tokens.shape
    n_experts = w_router.shape[1]
    n_clips, n_caps = teacher.shape
    hid = w_up.shape[1]
    n_dp = lax.axis_size("dp")
    n_exp = lax.axis_size("expert")
    caps_dp = n_caps // n_dp
    capacity = tok_rows // n_experts
    half = width // 2
    strip = width // n_exp
    rows = n_exp * capacity
    own = lax.axis_index("expert")
    own_dp = lax.axis_index("dp")
    at = jnp.stack([own // 2, own % 2, own_dp, own]).astype(jnp.int32)
    swap = [(i, i ^ 1) for i in range(n_exp)]
    router_t = w_router.T
    sds = jax.ShapeDtypeStruct

    def run(body, outs, operands, near=(), kept=(), scratch=(), flops=0):
        vmem = pl.BlockSpec(memory_space=pltpu.VMEM)
        hbm = pl.BlockSpec(memory_space=pltpu.HBM)
        late = [i for i, o in enumerate(operands) if o is not at and i not in near]
        leaving = [i for i in range(len(outs)) if i not in kept]

        def kernel(*refs):
            n_in, n_out = len(operands), len(outs)
            ins, results = list(refs[:n_in]), list(refs[n_in : n_in + n_out])
            rest = list(refs[n_in + n_out :])
            in_bufs, rest = rest[: len(late)], rest[len(late) :]
            out_bufs, rest = rest[: len(leaving)], rest[len(leaving) :]
            in_sems, out_sems, rest = rest[0], rest[1], rest[2:]
            for k, i in enumerate(late):
                ins[i] = Late(pltpu.make_async_copy(ins[i], in_bufs[k], in_sems.at[k]), in_bufs[k])
            for k, i in enumerate(leaving):
                results[i] = Leaving(
                    pltpu.make_async_copy(out_bufs[k], results[i], out_sems.at[k]), out_bufs[k]
                )
            body(*ins, *results, *rest)
            for i in late:
                ins[i].ready()
            for i in leaving:
                results[i].copy.wait()

        return pl.pallas_call(
            kernel,
            out_shape=outs,
            in_specs=[
                pl.BlockSpec(memory_space=pltpu.SMEM) if o is at else hbm if i in late else vmem
                for i, o in enumerate(operands)
            ],
            out_specs=[hbm if i in leaving else vmem for i in range(len(outs))],
            scratch_shapes=[pltpu.VMEM(operands[i].shape, operands[i].dtype) for i in late]
            + [pltpu.VMEM(outs[i].shape, outs[i].dtype) for i in leaving]
            + [
                pltpu.SemaphoreType.DMA((max(len(late), 1),)),
                pltpu.SemaphoreType.DMA((max(len(leaving), 1),)),
            ]
            + list(scratch),
            compiler_params=pltpu.CompilerParams(vmem_limit_bytes=64 * MIB),
            cost_estimate=pl.CostEstimate(flops=flops, bytes_accessed=0, transcendentals=0),
        )(*operands)

    send, base, placed = run(
        functools.partial(pack_kernel, capacity, n_experts, n_clips),
        [
            sds((n_experts, 2, capacity, half + LANES), bf16),
            sds((n_clips, width), f32),
            sds((tok_rows, n_experts * capacity), bf16),
        ],
        [routes.reshape(1, tok_rows), pool_ids, tokens],
        kept=(0, 1, 2),
    )
    recv = exchange(send.reshape(n_exp, capacity, half + LANES), "expert")
    start, _ = lax.optimization_barrier((captions, send))
    block = lax.ppermute(
        start,
        ("dp", "expert"),
        [(a * n_exp + b, (b * n_exp + a) if b < n_dp else a * n_exp + b) for a in range(n_dp) for b in range(n_exp)],
    )
    recv, block = lax.optimization_barrier((recv, block))
    other = lax.ppermute(recv, "expert", swap)
    gelu_slope, hidden, aux, counts, pay = run(
        functools.partial(forward_kernel, n_clips, strip),
        [
            sds((rows, hid), f32),
            sds((rows, hid), bf16),
            sds((rows, LANES), f32),
            sds((n_clips, LANES), f32),
            sds((n_exp // 2, 2, caps_dp, half + LANES), bf16),
        ],
        [at, recv, other, router_t, w_up, block, w_down, base],
        kept=(4,),
    )
    sums = exchange(pay.reshape(n_exp, caps_dp, half + LANES), "expert")
    (total,) = run(
        functools.partial(sum_kernel, strip),
        [sds((n_exp, n_clips, LANES), bf16)],
        [sums[:, :, half:]],
        kept=(0,),
    )
    total = exchange(total, "expert")
    other_sums = lax.ppermute(sums, "expert", swap)
    clip_grad, terms = run(
        functools.partial(loss_kernel, strip),
        [sds((n_clips, width), f32), sds((n_dp, caps_dp, LANES), f32)],
        [at, total, counts, sums, other_sums, clip_pairs.reshape(1, n_caps), teacher],
        near=(1,),
        scratch=[pltpu.VMEM((n_clips, width), f32)] * 3 + [pltpu.VMEM((n_caps, width), bf16)],
    )
    terms = exchange(terms, "dp")
    d_preact, dx_other, part = run(
        functools.partial(backward_kernel, n_clips),
        [sds((rows, hid), bf16), sds((rows, half), f32), sds((rows, LANES), f32)],
        [at, clip_grad, aux, w_down, gelu_slope, hidden, router_t, w_up],
        scratch=[pltpu.VMEM((rows + 2 * n_clips, width), bf16)],
    )
    from_other = lax.ppermute(dx_other, "expert", swap)
    (dx_own,) = run(
        own_kernel,
        [sds((rows, half), f32)],
        [at, d_preact, w_up, part, router_t],
        flops=OWN_FLOPS,
    )
    (pay,) = run(
        return_kernel,
        [sds((n_exp, capacity, half + LOW + LANES), bf16)],
        [dx_own, from_other, terms],
        kept=(0,),
    )
    back = exchange(pay, "expert")
    members = (pool_ids[0][:, None] == jnp.arange(n_clips, dtype=jnp.int32)[None, :]).astype(f32)
    token_dy = jnp.dot(members, clip_grad, precision=HIGHEST)
    token_grads, caption_grads = run(
        functools.partial(final_kernel, strip),
        [sds((tok_rows, width), f32), sds((caps_dp, width), f32)],
        [back.reshape(n_experts, 2, capacity, half + LOW + LANES), placed, token_dy],
        near=(0, 1, 2),
        kept=(0, 1),
    )
    return (token_grads, caption_grads)


def solution(mesh):
    return jax.shard_map(
        shards,
        mesh=mesh,
        in_specs=(
            P(("dp", "expert"), None),
            P(("dp", "expert"), None),
            P("dp", "expert"),
            P(),
            P(None, "expert"),
            P("expert", None),
            P("dp", None),
            P(),
            P("dp", None),
        ),
        out_specs=(P(("dp", "expert"), None), P("dp", None)),
        check_vma=False,
    )
```

```python
import functools
import jax
import jax.numpy as jnp
from jax import lax
from jax.experimental import pallas as pl
from jax.experimental.pallas import tpu as pltpu
from jax.sharding import PartitionSpec as P

HIGHEST = lax.Precision.HIGHEST
logit_scale = 10.0
logit_shift = -10.0
norm_eps = 1e-06
f32 = jnp.float32
bf16 = jnp.bfloat16
LANES = 128
MIB = 1 << 20
COVER = 10_000_000_000


def exchange(x, axis):
    return lax.all_to_all(x, axis, split_axis=0, concat_axis=0, tiled=True)


class Late:
    def __init__(self, copy, ref):
        self.copy, self.ref, self.begun, self.waited = copy, ref, False, False

    def begin(self):
        if not self.begun:
            self.copy.start()
            self.begun = True

    def ready(self):
        self.begin()
        if not self.waited:
            self.copy.wait()
            self.waited = True
        return self.ref


class Leaving:
    def __init__(self, copy, ref):
        self.copy, self.ref = copy, ref

    def send(self, value):
        self.ref[...] = value
        self.go()

    def go(self):
        self.copy.start()


def iota(shape, axis):
    return lax.broadcasted_iota(jnp.int32, shape, axis)


def nn(a, b):
    return lax.dot_general(a, b, (((1,), (0,)), ((), ())), preferred_element_type=f32)


def nt(a, b):
    return lax.dot_general(a, b, (((1,), (1,)), ((), ())), preferred_element_type=f32)


def stack3(x):
    high = x.astype(bf16).astype(f32)
    rest = x - high
    mid = rest.astype(bf16).astype(f32)
    return jnp.concatenate([high, mid, rest - mid], axis=0).astype(bf16)


def fold3(x):
    rows = x.shape[0] // 3
    return x[:rows] + (x[rows : 2 * rows] + x[2 * rows :])


def slot_matrix(route_row, capacity, n_experts):
    toks = route_row.shape[1]
    chosen = (iota((n_experts, toks), 0) == route_row).astype(f32)
    earlier = (iota((toks, toks), 0) < iota((toks, toks), 1)).astype(f32).astype(bf16)
    before = nn(chosen.astype(bf16), earlier)
    arrival = jnp.sum(before * chosen, axis=0, keepdims=True)
    slot = route_row.astype(f32) * capacity + arrival
    slot = jnp.where(arrival < capacity, slot, -1.0)
    return (iota((n_experts * capacity, toks), 0).astype(f32) == slot).astype(f32)


def pack_kernel(capacity, n_experts, n_clips, route, pool, tok, send_ref, base_ref, placed_ref):
    toks, width = tok.ref.shape
    half = width // 2
    placed_t = slot_matrix(route.ready()[...], capacity, n_experts)
    placed_ref[...] = placed_t.T.astype(bf16)
    placed_t = placed_t.astype(bf16)
    pool = pool.ready()[...]
    ids = iota((LANES, toks), 0)
    members = (ids == pool).astype(f32)
    counted = (ids - n_clips == pool).astype(f32).astype(bf16)
    side = nt(placed_t, members.astype(bf16)) + nt(
        jnp.ones((n_experts * capacity, toks), bf16), counted
    )
    side = side.reshape(n_experts, capacity, LANES).astype(bf16)
    tokens = tok.ready()[...]
    rows = nn(placed_t, tokens)
    for h in range(2):
        send_ref[:, h, :, :half] = (
            rows[:, h * half : (h + 1) * half].reshape(n_experts, capacity, half).astype(bf16)
        )
        send_ref[:, h, :, half:] = side
    base_ref[...] = nn(members[:n_clips].astype(bf16), tokens)


def cut_strip(tiles, e, strip):
    tile, offset = divmod(e * strip, LANES)
    lane = iota(tiles[0].shape, 1)
    value = tiles[tile]
    if offset + strip > LANES:
        value = jnp.where(lane >= offset, value, tiles[tile + 1])
    if offset:
        value = pltpu.roll(value, LANES - offset, 1)
    return jnp.where(lane < strip, value, 0.0)


def join_strips(strips, strip, n_tiles):
    lane = iota(strips[0].shape, 1)
    tiles = [jnp.zeros(strips[0].shape, f32) for _ in range(n_tiles)]
    for e, value in enumerate(strips):
        tile, offset = divmod(e * strip, LANES)
        if offset:
            value = pltpu.roll(value, offset, 1)
        if offset + strip > LANES:
            tiles[tile] = tiles[tile] + jnp.where(lane >= offset, value, 0.0)
            tiles[tile + 1] = tiles[tile + 1] + jnp.where(lane < offset, value, 0.0)
        else:
            tiles[tile] = tiles[tile] + value
    return tiles


def spread3(value, strip):
    high = value.astype(bf16).astype(f32)
    rest = value - high
    mid = rest.astype(bf16).astype(f32)
    return high + pltpu.roll(mid, strip, 1) + pltpu.roll(rest - mid, 2 * strip, 1)


def gather3(value, strip):
    lane = iota(value.shape, 1)
    low = pltpu.roll(value, LANES - 2 * strip, 1)
    mid = pltpu.roll(value, LANES - strip, 1)
    return jnp.where(lane < strip, value + (mid + low), 0.0)


def forward_kernel(
    n_clips, strip, at_ref, recv, other, router, up, block, down, base, slope, hidden_out, aux_out, counts, pay_ref,
):
    n_exp, capacity, wide = recv.ref.shape
    half = wide - LANES
    rows = n_exp * capacity
    n_experts = router.ref.shape[0]
    expert = at_ref[0]
    own_at = pl.multiple_of(at_ref[1] * half, LANES)
    other_at = pl.multiple_of((1 - at_ref[1]) * half, LANES)
    recv_ref = recv.ready()
    own = recv_ref[:, :, :half].astype(f32).reshape(rows, half).astype(bf16)
    side = recv_ref[:, :, half:].astype(f32).reshape(rows, LANES)
    other_rows = other.ready()[:, :, :half].astype(f32).reshape(rows, half).astype(bf16)
    router_ref = router.ready()
    scores = nt(own, router_ref[:, pl.ds(own_at, half)]) + nt(
        other_rows, router_ref[:, pl.ds(other_at, half)]
    )
    mine = iota((rows, n_experts), 1) == expert
    score = jnp.sum(jnp.where(mine, scores, 0.0), axis=1, keepdims=True)
    sigmoid_gate = jax.nn.sigmoid(score)
    gate = sigmoid_gate.astype(bf16).astype(f32)
    lane = iota((rows, LANES), 1)
    clip = jnp.where(lane < n_clips, side, 0.0)
    aux_out.send(
        jnp.where(
            lane == n_clips,
            gate,
            jnp.where(lane == n_clips + 1, sigmoid_gate * (1.0 - sigmoid_gate), clip),
        )
    )
    side_t = side.T
    counts.send(
        jnp.broadcast_to(
            jnp.sum(side_t[n_clips : 2 * n_clips], axis=1, keepdims=True) / capacity,
            (n_clips, LANES),
        )
    )
    weights = (clip * gate).T[:n_clips].astype(bf16)
    up_ref = up.ready()
    down.begin()
    block.begin()
    base.begin()
    preact = nn(own, up_ref[pl.ds(own_at, half), :]) + nn(
        other_rows, up_ref[pl.ds(other_at, half), :]
    )
    root = 0.7978845608028654
    square = preact * preact
    tanh = jnp.tanh(root * (preact + 0.044715 * (square * preact)))
    hidden = (preact * (0.5 * (1.0 + tanh))).astype(bf16)
    hidden_out.send(hidden)
    slope.send(
        0.5 * (1.0 + tanh)
        + 0.5 * preact * (1.0 - tanh * tanh) * (root * (1.0 + (3 * 0.044715) * square))
    )
    captions = block.ready()
    for h in range(2):
        pay_ref[:, h, :, :half] = jnp.broadcast_to(
            captions[:, h * half : (h + 1) * half][None], (n_exp // 2, captions.shape[0], half)
        )
    produced = nn(hidden, down.ready()[...])
    high = produced.astype(bf16)
    low = (produced - high.astype(f32)).astype(bf16)
    pooled = base.ready()[...] + (nn(weights, high) + nn(weights, low))
    tiles = [pooled[:, t * LANES : (t + 1) * LANES] for t in range(pooled.shape[1] // LANES)]
    for e in range(n_exp):
        pay_ref[e // 2, e % 2, :, half:] = spread3(cut_strip(tiles, e, strip), strip).astype(bf16)


def sum_kernel(strip, side, out_ref):
    total = jnp.sum(side.ready()[...].astype(f32), axis=0)
    total = spread3(gather3(total, strip), strip).astype(bf16)
    out_ref[...] = jnp.broadcast_to(total[None], out_ref.shape)


def text_kernel(strip, at_ref, own, other, pairs, teacher, text_out, table_out, strip_out):
    n_clips, n_caps = teacher.ref.shape
    half = own.ref.shape[2]
    width = 2 * half
    own_at = pl.multiple_of(at_ref[1] * half, LANES)
    other_at = pl.multiple_of((1 - at_ref[1]) * half, LANES)
    matched = (
        pairs.ready()[...] == at_ref[2] * n_clips + iota((n_clips, n_caps), 0)
    ).astype(f32)
    target = 0.5 * matched + 0.5 * jax.nn.sigmoid(teacher.ready()[...])
    own_text = own.ready()[...].astype(f32).reshape(n_caps, half)
    other_text = other.ready()[...].astype(f32).reshape(n_caps, half)
    text_out.ref[:, pl.ds(own_at, half)] = own_text.astype(bf16)
    text_out.ref[:, pl.ds(other_at, half)] = other_text.astype(bf16)
    text_out.go()
    ones = jnp.ones((16, half), bf16)

    def squares(text):
        square = text * text
        high = square.astype(bf16)
        return nt(ones, high) + nt(ones, (square - high.astype(f32)).astype(bf16))

    text_scale = lax.rsqrt((squares(own_text) + squares(other_text))[:n_clips] + norm_eps)
    table_out.send(jnp.concatenate([text_scale, target], axis=0))
    pick = (
        (iota((width, LANES), 0) - at_ref[3] * strip == iota((width, LANES), 1))
        & (iota((width, LANES), 1) < strip)
    ).astype(f32).astype(bf16)
    strip_out.send(nn(text_out.ref[...], pick))


def loss_kernel(
    strip, at_ref, sums_ref, counts, table, text, raw_strip, grad_out, terms_out, mean_ref,
):
    n_exp, n_clips, _ = sums_ref.shape
    n_caps, width = text.ref.shape
    n_tiles = width // LANES
    tiles = join_strips(
        [gather3(sums_ref[e].astype(f32), strip) for e in range(n_exp)], strip, n_tiles
    )
    counts = counts.ready()[:, :1]
    for t, tile in enumerate(tiles):
        mean_ref[:, t * LANES : (t + 1) * LANES] = tile / counts
    clip_mean = mean_ref[...]
    img_scale = lax.rsqrt(jnp.sum(clip_mean * clip_mean, axis=1, keepdims=True) + norm_eps)
    image_emb = clip_mean * img_scale
    text = text.ready()[...]
    raw = fold3(nt(stack3(image_emb), text))
    table = table.ready()[...]
    text_scale = table[:n_clips]
    logits = logit_scale * raw * text_scale + logit_shift
    loss_grad = (jax.nn.sigmoid(logits) - table[n_clips:]) * (counts / n_caps)
    scaled = loss_grad * text_scale
    d_image = logit_scale * fold3(nn(stack3(scaled), text))
    mean_grad = (
        img_scale * d_image
        - img_scale
        * img_scale
        * img_scale
        * jnp.sum(clip_mean * d_image, axis=1, keepdims=True)
        * clip_mean
    )
    grad_out.send(mean_grad / counts)
    emb_strip = gather3(sums_ref[at_ref[3]].astype(f32), strip) / counts * img_scale
    dots = jnp.sum(loss_grad * raw, axis=0, keepdims=True)
    cube = text_scale[:1] * text_scale[:1] * text_scale[:1] * dots
    both = jnp.concatenate([scaled, jnp.broadcast_to(cube, scaled.shape)], axis=0)
    both = jnp.concatenate([both, jnp.zeros((LANES - both.shape[0], n_caps), f32)], axis=0).T
    products = lax.dot_general(
        both[:, :n_clips], emb_strip, (((1,), (0,)), ((), ())),
        precision=HIGHEST, preferred_element_type=f32,
    )
    terms = logit_scale * (products - both[:, n_clips : n_clips + 1] * raw_strip.ready()[...])
    terms_out.send(terms.reshape(terms_out.ref.shape))


def backward_kernel(
    n_clips, at_ref, grad, aux, down, slope, hidden, router, up,
    d_preact_out, out, part_out, stacked_ref,
):
    rows, hid = hidden.ref.shape
    width = grad.ref.shape[1]
    half = width // 2
    expert = at_ref[0]
    other_at = pl.multiple_of((1 - at_ref[1]) * half, LANES)
    grads = grad.ready()[...]
    aux = aux.ready()[...]
    lane = iota((rows, LANES), 1)
    clip = jnp.sum(jnp.where(lane < n_clips, aux * lane.astype(f32), 0.0), axis=1, keepdims=True)
    gate = aux[:, n_clips : n_clips + 1]
    gate_slope = aux[:, n_clips + 1 : n_clips + 2]
    lane3 = lane % n_clips
    thrice = ((lane3.astype(f32) == clip) & (lane < 3 * n_clips)).astype(f32).astype(bf16)
    high = grads.astype(bf16).astype(f32)
    rest = grads - high
    mid = rest.astype(bf16).astype(f32)
    parts = jnp.concatenate(
        [high, mid, rest - mid, jnp.zeros((LANES - 3 * n_clips, width), f32)], axis=0
    ).astype(bf16)
    unit_dy = nn(thrice, parts)
    down.ready()
    slope.begin()
    hidden.begin()
    router.begin()
    up.begin()
    stacked_ref[:rows, :] = (gate * unit_dy).astype(bf16)
    stacked_ref[rows:, :] = jnp.concatenate([high, mid], axis=0).astype(bf16)
    d_all = nt(stacked_ref[...], down.ready()[...])
    d_preact = (d_all[:rows] * slope.ready()[...]).astype(bf16)
    d_preact_out.send(d_preact)
    by_clip = d_all[rows : rows + n_clips] + d_all[rows + n_clips :]
    high_v = by_clip.astype(bf16).astype(f32)
    two = jnp.concatenate([high_v, by_clip - high_v], axis=0).astype(bf16)
    dots = nt(hidden.ready()[...], two)
    lane2 = iota((rows, 2 * n_clips), 1) % n_clips
    token_dg = jnp.sum(
        jnp.where(lane2.astype(f32) == clip, dots, 0.0), axis=1, keepdims=True
    )
    part = token_dg * gate_slope
    part_out.send(jnp.broadcast_to(part, (rows, LANES)))
    router = jnp.sum(
        jnp.where(
            iota((router.ref.shape[0], half), 0) == expert,
            router.ready()[:, pl.ds(other_at, half)].astype(f32),
            0.0,
        ),
        axis=0,
        keepdims=True,
    )
    out.send(nt(d_preact, up.ready()[...]) + part * router)


def own_kernel(at_ref, d_preact, up, part, router, out):
    half = out.ref.shape[1]
    expert = at_ref[0]
    own_at = pl.multiple_of(at_ref[1] * half, LANES)
    router = jnp.sum(
        jnp.where(
            iota((router.ref.shape[0], half), 0) == expert,
            router.ready()[:, pl.ds(own_at, half)].astype(f32),
            0.0,
        ),
        axis=0,
        keepdims=True,
    )
    out.send(
        nt(d_preact.ready()[...], up.ready()[...])
        + part.ready()[:, :1] * router
    )


def return_kernel(own, other, terms, pay_ref):
    n_exp, capacity, _ = pay_ref.shape
    half = own.ref.shape[1]
    strip = jnp.sum(terms.ready()[...], axis=0)
    strip_high = strip.astype(bf16).astype(f32)
    side = strip_high + pltpu.roll(strip - strip_high, LANES // 2, 1)
    pay_ref[:, :, half:] = jnp.broadcast_to(
        side.astype(bf16)[None], (n_exp, capacity, LANES)
    )
    total = (own.ready()[...] + other.ready()[...]).reshape(n_exp, capacity, half)
    pay_ref[:, :, :half] = total.astype(bf16)


def final_kernel(strip, back_ref, placed_ref, dy_ref, out_ref, caps_ref):
    n_experts, _, capacity, wide = back_ref.shape
    half = wide - LANES
    placed = placed_ref[...]
    slots = n_experts * capacity

    for h in range(2):
        part = back_ref[:, h, :, :half].astype(f32).reshape(slots, half).astype(bf16)
        out_ref[:, h * half : (h + 1) * half] = (
            dy_ref[:, h * half : (h + 1) * half] + nn(placed, part)
        )
    lane = iota((capacity, LANES), 1)
    strips = []
    for e in range(2 * n_experts):
        side = back_ref[e // 2, e % 2, :, half:].astype(f32)
        strips.append(jnp.where(lane < strip, side + pltpu.roll(side, LANES // 2, 1), 0.0))
    for t, value in enumerate(join_strips(strips, strip, caps_ref.shape[1] // LANES)):
        caps_ref[:, t * LANES : (t + 1) * LANES] = value


def shards(tokens, routes, pool_ids, w_router, w_up, w_down, captions, clip_pairs, teacher):
    tok_rows, width = tokens.shape
    n_experts = w_router.shape[1]
    n_clips, n_caps = teacher.shape
    hid = w_up.shape[1]
    n_dp = lax.axis_size("dp")
    n_exp = lax.axis_size("expert")
    caps_dp = n_caps // n_dp
    capacity = tok_rows // n_experts
    half = width // 2
    strip = width // n_exp
    rows = n_exp * capacity
    own = lax.axis_index("expert")
    own_dp = lax.axis_index("dp")
    at = jnp.stack([own // 2, own % 2, own_dp, own]).astype(jnp.int32)
    swap = [(i, i ^ 1) for i in range(n_exp)]
    router_t = w_router.T
    sds = jax.ShapeDtypeStruct

    def run(body, outs, operands, near=(), kept=(), held=(), views=(), scratch=(), flops=0):
        views = dict(views)
        vmem = pl.BlockSpec(memory_space=pltpu.VMEM)
        hbm = pl.BlockSpec(memory_space=pltpu.HBM)
        late = [i for i, o in enumerate(operands) if o is not at and i not in near]
        leaving = [i for i in range(len(outs)) if i not in kept]

        def kernel(*refs):
            n_in, n_out = len(operands), len(outs)
            ins, results = list(refs[:n_in]), list(refs[n_in : n_in + n_out])
            rest = list(refs[n_in + n_out :])
            in_bufs, rest = rest[: len(late)], rest[len(late) :]
            out_bufs, rest = rest[: len(leaving)], rest[len(leaving) :]
            in_sems, out_sems, rest = rest[0], rest[1], rest[2:]
            for k, i in enumerate(late):
                source = views[i][1](ins[i], ins[0]) if i in views else ins[i]
                ins[i] = Late(pltpu.make_async_copy(source, in_bufs[k], in_sems.at[k]), in_bufs[k])
                if i not in held:
                    ins[i].begin()
            for k, i in enumerate(leaving):
                results[i] = Leaving(
                    pltpu.make_async_copy(out_bufs[k], results[i], out_sems.at[k]), out_bufs[k]
                )
            body(*ins, *results, *rest)
            for i in late:
                ins[i].ready()
            for i in leaving:
                results[i].copy.wait()

        return pl.pallas_call(
            kernel,
            out_shape=outs,
            in_specs=[
                pl.BlockSpec(memory_space=pltpu.SMEM) if o is at else hbm if i in late else vmem
                for i, o in enumerate(operands)
            ],
            out_specs=[hbm if i in leaving else vmem for i in range(len(outs))],
            scratch_shapes=[
                pltpu.VMEM(views[i][0] if i in views else operands[i].shape, operands[i].dtype)
                for i in late
            ]
            + [pltpu.VMEM(outs[i].shape, outs[i].dtype) for i in leaving]
            + [
                pltpu.SemaphoreType.DMA((max(len(late), 1),)),
                pltpu.SemaphoreType.DMA((max(len(leaving), 1),)),
            ]
            + list(scratch),
            compiler_params=pltpu.CompilerParams(vmem_limit_bytes=64 * MIB),
            cost_estimate=pl.CostEstimate(flops=flops, bytes_accessed=0, transcendentals=0),
        )(*operands)

    def up_rows(flip):
        def cut(ref, at_ref):
            return ref.at[pl.ds(pl.multiple_of((at_ref[1] ^ flip) * half, LANES), half), :]

        return ((half, hid), cut)

    send, base, placed = run(
        functools.partial(pack_kernel, capacity, n_experts, n_clips),
        [
            sds((n_experts, 2, capacity, half + LANES), bf16),
            sds((n_clips, width), f32),
            sds((tok_rows, n_experts * capacity), bf16),
        ],
        [routes.reshape(1, tok_rows), pool_ids, tokens],
        kept=(0, 1, 2),
    )
    recv = exchange(send.reshape(n_exp, capacity, half + LANES), "expert")
    start, _ = lax.optimization_barrier((captions, send))
    block = lax.ppermute(
        start,
        ("dp", "expert"),
        [(a * n_exp + b, (b * n_exp + a) if b < n_dp else a * n_exp + b) for a in range(n_dp) for b in range(n_exp)],
    )
    recv, block = lax.optimization_barrier((recv, block))
    other = lax.ppermute(recv, "expert", swap)
    gelu_slope, hidden, aux, counts, pay = run(
        functools.partial(forward_kernel, n_clips, strip),
        [
            sds((rows, hid), f32),
            sds((rows, hid), bf16),
            sds((rows, LANES), f32),
            sds((n_clips, LANES), f32),
            sds((n_exp // 2, 2, caps_dp, half + LANES), bf16),
        ],
        [at, recv, other, router_t, w_up, block, w_down, base],
        kept=(4,),
        held=(5, 6, 7),
    )
    sums = exchange(pay.reshape(n_exp, caps_dp, half + LANES), "expert")
    (total,) = run(
        functools.partial(sum_kernel, strip),
        [sds((n_exp, n_clips, LANES), bf16)],
        [sums],
        kept=(0,),
        views={0: ((n_exp, caps_dp, LANES), lambda ref, _: ref.at[:, :, pl.ds(half, LANES)])},
    )
    total = exchange(total, "expert")
    other_sums = lax.ppermute(sums, "expert", swap)
    cut_text = ((n_exp, caps_dp, half), lambda ref, _: ref.at[:, :, pl.ds(0, half)])
    text, table, raw_strip = run(
        functools.partial(text_kernel, strip),
        [
            sds((n_caps, width), bf16),
            sds((2 * n_clips, n_caps), f32),
            sds((n_caps, LANES), f32),
        ],
        [at, sums, other_sums, clip_pairs.reshape(1, n_caps), teacher],
        views={1: cut_text, 2: cut_text},
        flops=COVER,
    )
    clip_grad, terms = run(
        functools.partial(loss_kernel, strip),
        [sds((n_clips, width), f32), sds((n_dp, caps_dp, LANES), f32)],
        [at, total, counts, table, text, raw_strip],
        near=(1,),
        scratch=[pltpu.VMEM((n_clips, width), f32)],
    )
    terms = exchange(terms, "dp")
    d_preact, dx_other, part = run(
        functools.partial(backward_kernel, n_clips),
        [sds((rows, hid), bf16), sds((rows, half), f32), sds((rows, LANES), f32)],
        [at, clip_grad, aux, w_down, gelu_slope, hidden, router_t, w_up],
        held=(4, 5, 6, 7),
        views={7: up_rows(1)},
        scratch=[pltpu.VMEM((rows + 2 * n_clips, width), bf16)],
    )
    from_other = lax.ppermute(dx_other, "expert", swap)
    (dx_own,) = run(
        own_kernel,
        [sds((rows, half), f32)],
        [at, d_preact, w_up, part, router_t],
        views={2: up_rows(0)},
        flops=COVER,
    )
    (pay,) = run(
        return_kernel,
        [sds((n_exp, capacity, half + LANES), bf16)],
        [dx_own, from_other, terms],
        kept=(0,),
    )
    back = exchange(pay, "expert")
    members = (pool_ids[0][:, None] == jnp.arange(n_clips, dtype=jnp.int32)[None, :]).astype(f32)
    token_dy = jnp.dot(members, clip_grad, precision=HIGHEST)
    token_grads, caption_grads = run(
        functools.partial(final_kernel, strip),
        [sds((tok_rows, width), f32), sds((caps_dp, width), f32)],
        [back.reshape(n_experts, 2, capacity, half + LANES), placed, token_dy],
        near=(0, 1, 2),
        kept=(0, 1),
    )
    return (token_grads, caption_grads)


def solution(mesh):
    return jax.shard_map(
        shards,
        mesh=mesh,
        in_specs=(
            P(("dp", "expert"), None),
            P(("dp", "expert"), None),
            P("dp", "expert"),
            P(),
            P(None, "expert"),
            P("expert", None),
            P("dp", None),
            P(),
            P("dp", None),
        ),
        out_specs=(P(("dp", "expert"), None), P("dp", None)),
        check_vma=False,
    )
```

```python
import functools
import jax
import jax.numpy as jnp
from jax import lax
from jax.experimental import pallas as pl
from jax.experimental.pallas import tpu as pltpu
from jax.sharding import PartitionSpec as P

HIGHEST = lax.Precision.HIGHEST
logit_scale = 10.0
logit_shift = -10.0
norm_eps = 1e-06
f32 = jnp.float32
bf16 = jnp.bfloat16
LANES = 128
MIB = 1 << 20
COVER = 10_000_000_000


def exchange(x, axis):
    return lax.all_to_all(x, axis, split_axis=0, concat_axis=0, tiled=True)


class Late:
    def __init__(self, copy, ref):
        self.copy, self.ref, self.waited = copy, ref, False
        copy.start()

    def ready(self):
        if not self.waited:
            self.copy.wait()
            self.waited = True
        return self.ref


class Leaving:
    def __init__(self, copy, ref):
        self.copy, self.ref, self.sent = copy, ref, False

    def send(self, value):
        self.ref[...] = value
        self.copy.start()
        self.sent = True


def iota(shape, axis):
    return lax.broadcasted_iota(jnp.int32, shape, axis)


def nn(a, b):
    return lax.dot_general(a, b, (((1,), (0,)), ((), ())), preferred_element_type=f32)


def nt(a, b):
    return lax.dot_general(a, b, (((1,), (1,)), ((), ())), preferred_element_type=f32)


def stack3(x):
    high = x.astype(bf16).astype(f32)
    rest = x - high
    mid = rest.astype(bf16).astype(f32)
    return jnp.concatenate([high, mid, rest - mid], axis=0).astype(bf16)


def fold3(x):
    rows = x.shape[0] // 3
    return x[:rows] + (x[rows : 2 * rows] + x[2 * rows :])


def slot_matrix(route_row, capacity, n_experts):
    toks = route_row.shape[1]
    chosen = (iota((n_experts, toks), 0) == route_row).astype(f32)
    earlier = (iota((toks, toks), 0) < iota((toks, toks), 1)).astype(f32).astype(bf16)
    before = nn(chosen.astype(bf16), earlier)
    arrival = jnp.sum(before * chosen, axis=0, keepdims=True)
    slot = route_row.astype(f32) * capacity + arrival
    slot = jnp.where(arrival < capacity, slot, -1.0)
    return (iota((n_experts * capacity, toks), 0).astype(f32) == slot).astype(f32)


def pack_kernel(capacity, n_experts, n_clips, route, pool, tok, send_ref, base_ref, placed_ref):
    toks, width = tok.ref.shape
    half = width // 2
    placed_t = slot_matrix(route.ready()[...], capacity, n_experts)
    placed_ref[...] = placed_t.T.astype(bf16)
    placed_t = placed_t.astype(bf16)
    pool = pool.ready()[...]
    ids = iota((LANES, toks), 0)
    members = (ids == pool).astype(f32)
    counted = (ids - n_clips == pool).astype(f32).astype(bf16)
    side = nt(placed_t, members.astype(bf16)) + nt(
        jnp.ones((n_experts * capacity, toks), bf16), counted
    )
    side = side.reshape(n_experts, capacity, LANES).astype(bf16)
    tokens = tok.ready()[...]
    rows = nn(placed_t, tokens)
    for h in range(2):
        send_ref[:, h, :, :half] = (
            rows[:, h * half : (h + 1) * half].reshape(n_experts, capacity, half).astype(bf16)
        )
        send_ref[:, h, :, half:] = side
    base_ref[...] = nn(members[:n_clips].astype(bf16), tokens)


def cut_strip(tiles, e, strip):
    tile, offset = divmod(e * strip, LANES)
    lane = iota(tiles[0].shape, 1)
    value = tiles[tile]
    if offset + strip > LANES:
        value = jnp.where(lane >= offset, value, tiles[tile + 1])
    if offset:
        value = pltpu.roll(value, LANES - offset, 1)
    return jnp.where(lane < strip, value, 0.0)


def join_strips(strips, strip, n_tiles):
    lane = iota(strips[0].shape, 1)
    tiles = [jnp.zeros(strips[0].shape, f32) for _ in range(n_tiles)]
    for e, value in enumerate(strips):
        tile, offset = divmod(e * strip, LANES)
        if offset:
            value = pltpu.roll(value, offset, 1)
        if offset + strip > LANES:
            tiles[tile] = tiles[tile] + jnp.where(lane >= offset, value, 0.0)
            tiles[tile + 1] = tiles[tile + 1] + jnp.where(lane < offset, value, 0.0)
        else:
            tiles[tile] = tiles[tile] + value
    return tiles


def spread3(value, strip):
    high = value.astype(bf16).astype(f32)
    rest = value - high
    mid = rest.astype(bf16).astype(f32)
    return high + pltpu.roll(mid, strip, 1) + pltpu.roll(rest - mid, 2 * strip, 1)


def gather3(value, strip):
    lane = iota(value.shape, 1)
    low = pltpu.roll(value, LANES - 2 * strip, 1)
    mid = pltpu.roll(value, LANES - strip, 1)
    return jnp.where(lane < strip, value + (mid + low), 0.0)


def forward_kernel(
    n_clips, strip, at_ref, recv, other, router, up, block, down, base, slope, hidden_out, aux_out, counts, pay_ref,
):
    n_exp, capacity, wide = recv.ref.shape
    half = wide - LANES
    rows = n_exp * capacity
    n_experts = router.ref.shape[0]
    expert = at_ref[0]
    own_at = pl.multiple_of(at_ref[1] * half, LANES)
    other_at = pl.multiple_of((1 - at_ref[1]) * half, LANES)
    recv_ref = recv.ready()
    own = recv_ref[:, :, :half].astype(f32).reshape(rows, half).astype(bf16)
    side = recv_ref[:, :, half:].astype(f32).reshape(rows, LANES)
    other_rows = other.ready()[:, :, :half].astype(f32).reshape(rows, half).astype(bf16)
    router_ref = router.ready()
    scores = nt(own, router_ref[:, pl.ds(own_at, half)]) + nt(
        other_rows, router_ref[:, pl.ds(other_at, half)]
    )
    mine = iota((rows, n_experts), 1) == expert
    score = jnp.sum(jnp.where(mine, scores, 0.0), axis=1, keepdims=True)
    sigmoid_gate = jax.nn.sigmoid(score)
    gate = sigmoid_gate.astype(bf16).astype(f32)
    lane = iota((rows, LANES), 1)
    clip = jnp.where(lane < n_clips, side, 0.0)
    aux_out.send(
        jnp.where(
            lane == n_clips,
            gate,
            jnp.where(lane == n_clips + 1, sigmoid_gate * (1.0 - sigmoid_gate), clip),
        )
    )
    side_t = side.T
    counts.send(
        jnp.broadcast_to(
            jnp.sum(side_t[n_clips : 2 * n_clips], axis=1, keepdims=True) / capacity,
            (n_clips, LANES),
        )
    )
    weights = (clip * gate).T[:n_clips].astype(bf16)
    up_ref = up.ready()
    preact = nn(own, up_ref[pl.ds(own_at, half), :]) + nn(
        other_rows, up_ref[pl.ds(other_at, half), :]
    )
    root = 0.7978845608028654
    square = preact * preact
    tanh = jnp.tanh(root * (preact + 0.044715 * (square * preact)))
    hidden = (preact * (0.5 * (1.0 + tanh))).astype(bf16)
    hidden_out.send(hidden)
    slope.send(
        0.5 * (1.0 + tanh)
        + 0.5 * preact * (1.0 - tanh * tanh) * (root * (1.0 + (3 * 0.044715) * square))
    )
    captions = block.ready()
    for h in range(2):
        pay_ref[:, h, :, :half] = jnp.broadcast_to(
            captions[:, h * half : (h + 1) * half][None], (n_exp // 2, captions.shape[0], half)
        )
    produced = nn(hidden, down.ready()[...])
    high = produced.astype(bf16)
    low = (produced - high.astype(f32)).astype(bf16)
    pooled = base.ready()[...] + (nn(weights, high) + nn(weights, low))
    tiles = [pooled[:, t * LANES : (t + 1) * LANES] for t in range(pooled.shape[1] // LANES)]
    for e in range(n_exp):
        pay_ref[e // 2, e % 2, :, half:] = spread3(cut_strip(tiles, e, strip), strip).astype(bf16)


def sum_kernel(strip, side, out_ref):
    total = jnp.sum(side.ready()[...].astype(f32), axis=0)
    total = spread3(gather3(total, strip), strip).astype(bf16)
    out_ref[...] = jnp.broadcast_to(total[None], out_ref.shape)


def loss_kernel(
    strip, at_ref, sums_ref, counts, own, other, pairs, teacher, grad_out, terms_out,
    mean_ref, image_ref, d_image_ref, text_ref,
):
    n_exp, n_clips, wide = own.ref.shape
    n_caps = teacher.ref.shape[1]
    half = wide - LANES
    width = 2 * half
    own_at = pl.multiple_of(at_ref[1] * half, LANES)
    other_at = pl.multiple_of((1 - at_ref[1]) * half, LANES)
    own_dp = at_ref[2]
    n_tiles = width // LANES
    tiles = join_strips(
        [gather3(sums_ref[e].astype(f32), strip) for e in range(n_exp)], strip, n_tiles
    )
    counts = counts.ready()[:, :1]
    for t, tile in enumerate(tiles):
        mean_ref[:, t * LANES : (t + 1) * LANES] = tile / counts
    clip_mean = mean_ref[...]
    img_scale = lax.rsqrt(jnp.sum(clip_mean * clip_mean, axis=1, keepdims=True) + norm_eps)
    image_emb = clip_mean * img_scale
    image_ref[...] = image_emb
    own_text = own.ready()[:, :, :half].astype(f32).reshape(n_caps, half)
    other_text = other.ready()[:, :, :half].astype(f32).reshape(n_caps, half)
    ones = jnp.ones((16, half), bf16)

    def squares(text):
        square = text * text
        high = square.astype(bf16)
        return nt(ones, high) + nt(ones, (square - high.astype(f32)).astype(bf16))

    text_scale = lax.rsqrt((squares(own_text) + squares(other_text))[:n_clips] + norm_eps)
    own_text = own_text.astype(bf16)
    other_text = other_text.astype(bf16)
    text_ref[:, pl.ds(own_at, half)] = own_text
    text_ref[:, pl.ds(other_at, half)] = other_text
    text = text_ref[...]
    raw = fold3(nt(stack3(image_emb), text))
    matched = (
        pairs.ready()[...] == own_dp * n_clips + iota((n_clips, n_caps), 0)
    ).astype(f32)
    target = 0.5 * matched + 0.5 * jax.nn.sigmoid(teacher.ready()[...])
    logits = logit_scale * raw * text_scale + logit_shift
    loss_grad = (jax.nn.sigmoid(logits) - target) * (counts / n_caps)
    scaled = loss_grad * text_scale
    d_image = logit_scale * fold3(nn(stack3(scaled), text))
    mean_grad = (
        img_scale * d_image
        - img_scale
        * img_scale
        * img_scale
        * jnp.sum(clip_mean * d_image, axis=1, keepdims=True)
        * clip_mean
    )
    grad_out.send(mean_grad / counts)
    pick = (
        (iota((width, LANES), 0) - at_ref[3] * strip == iota((width, LANES), 1))
        & (iota((width, LANES), 1) < strip)
    ).astype(f32).astype(bf16)
    emb_strip = fold3(nn(stack3(image_emb), pick))
    raw_strip = nn(text, pick)
    dots = jnp.sum(loss_grad * raw, axis=0, keepdims=True)
    cube = text_scale[:1] * text_scale[:1] * text_scale[:1] * dots
    both = jnp.concatenate([scaled, jnp.broadcast_to(cube, scaled.shape)], axis=0)
    both = jnp.concatenate([both, jnp.zeros((LANES - both.shape[0], n_caps), f32)], axis=0).T
    products = lax.dot_general(
        both[:, :n_clips], emb_strip, (((1,), (0,)), ((), ())),
        precision=HIGHEST, preferred_element_type=f32,
    )
    terms = logit_scale * (products - both[:, n_clips : n_clips + 1] * raw_strip)
    terms_out.send(terms.reshape(terms_out.ref.shape))


def backward_kernel(
    n_clips, at_ref, grad, aux, down, slope, hidden, router, up,
    d_preact_out, out, part_out, stacked_ref,
):
    rows, hid = hidden.ref.shape
    width = grad.ref.shape[1]
    half = width // 2
    expert = at_ref[0]
    other_at = pl.multiple_of((1 - at_ref[1]) * half, LANES)
    grads = grad.ready()[...]
    aux = aux.ready()[...]
    lane = iota((rows, LANES), 1)
    clip = jnp.sum(jnp.where(lane < n_clips, aux * lane.astype(f32), 0.0), axis=1, keepdims=True)
    gate = aux[:, n_clips : n_clips + 1]
    gate_slope = aux[:, n_clips + 1 : n_clips + 2]
    lane3 = lane % n_clips
    thrice = ((lane3.astype(f32) == clip) & (lane < 3 * n_clips)).astype(f32).astype(bf16)
    high = grads.astype(bf16).astype(f32)
    rest = grads - high
    mid = rest.astype(bf16).astype(f32)
    parts = jnp.concatenate(
        [high, mid, rest - mid, jnp.zeros((LANES - 3 * n_clips, width), f32)], axis=0
    ).astype(bf16)
    unit_dy = nn(thrice, parts)
    stacked_ref[:rows, :] = (gate * unit_dy).astype(bf16)
    stacked_ref[rows:, :] = jnp.concatenate([high, mid], axis=0).astype(bf16)
    d_all = nt(stacked_ref[...], down.ready()[...])
    d_preact = (d_all[:rows] * slope.ready()[...]).astype(bf16)
    d_preact_out.send(d_preact)
    by_clip = d_all[rows : rows + n_clips] + d_all[rows + n_clips :]
    high_v = by_clip.astype(bf16).astype(f32)
    two = jnp.concatenate([high_v, by_clip - high_v], axis=0).astype(bf16)
    dots = nt(hidden.ready()[...], two)
    lane2 = iota((rows, 2 * n_clips), 1) % n_clips
    token_dg = jnp.sum(
        jnp.where(lane2.astype(f32) == clip, dots, 0.0), axis=1, keepdims=True
    )
    part = token_dg * gate_slope
    part_out.send(jnp.broadcast_to(part, (rows, LANES)))
    router = jnp.sum(
        jnp.where(
            iota((router.ref.shape[0], half), 0) == expert,
            router.ready()[:, pl.ds(other_at, half)].astype(f32),
            0.0,
        ),
        axis=0,
        keepdims=True,
    )
    out.send(nt(d_preact, up.ready()[...]) + part * router)


def own_kernel(at_ref, d_preact, up, part, router, out):
    half = out.ref.shape[1]
    expert = at_ref[0]
    own_at = pl.multiple_of(at_ref[1] * half, LANES)
    router = jnp.sum(
        jnp.where(
            iota((router.ref.shape[0], half), 0) == expert,
            router.ready()[:, pl.ds(own_at, half)].astype(f32),
            0.0,
        ),
        axis=0,
        keepdims=True,
    )
    out.send(
        nt(d_preact.ready()[...], up.ready()[...])
        + part.ready()[:, :1] * router
    )


def return_kernel(own, other, terms, pay_ref):
    n_exp, capacity, _ = pay_ref.shape
    half = own.ref.shape[1]
    strip = jnp.sum(terms.ready()[...], axis=0)
    strip_high = strip.astype(bf16).astype(f32)
    side = strip_high + pltpu.roll(strip - strip_high, LANES // 2, 1)
    pay_ref[:, :, half:] = jnp.broadcast_to(
        side.astype(bf16)[None], (n_exp, capacity, LANES)
    )
    total = (own.ready()[...] + other.ready()[...]).reshape(n_exp, capacity, half)
    pay_ref[:, :, :half] = total.astype(bf16)


def final_kernel(strip, back_ref, placed_ref, dy_ref, out_ref, caps_ref):
    n_experts, _, capacity, wide = back_ref.shape
    half = wide - LANES
    placed = placed_ref[...]
    slots = n_experts * capacity

    for h in range(2):
        part = back_ref[:, h, :, :half].astype(f32).reshape(slots, half).astype(bf16)
        out_ref[:, h * half : (h + 1) * half] = (
            dy_ref[:, h * half : (h + 1) * half] + nn(placed, part)
        )
    lane = iota((capacity, LANES), 1)
    strips = []
    for e in range(2 * n_experts):
        side = back_ref[e // 2, e % 2, :, half:].astype(f32)
        strips.append(jnp.where(lane < strip, side + pltpu.roll(side, LANES // 2, 1), 0.0))
    for t, value in enumerate(join_strips(strips, strip, caps_ref.shape[1] // LANES)):
        caps_ref[:, t * LANES : (t + 1) * LANES] = value


def shards(tokens, routes, pool_ids, w_router, w_up, w_down, captions, clip_pairs, teacher):
    tok_rows, width = tokens.shape
    n_experts = w_router.shape[1]
    n_clips, n_caps = teacher.shape
    hid = w_up.shape[1]
    n_dp = lax.axis_size("dp")
    n_exp = lax.axis_size("expert")
    caps_dp = n_caps // n_dp
    capacity = tok_rows // n_experts
    half = width // 2
    strip = width // n_exp
    rows = n_exp * capacity
    own = lax.axis_index("expert")
    own_dp = lax.axis_index("dp")
    at = jnp.stack([own // 2, own % 2, own_dp, own]).astype(jnp.int32)
    swap = [(i, i ^ 1) for i in range(n_exp)]
    router_t = w_router.T
    sds = jax.ShapeDtypeStruct

    def run(body, outs, operands, near=(), kept=(), views=(), scratch=(), flops=0):
        views = dict(views)
        vmem = pl.BlockSpec(memory_space=pltpu.VMEM)
        hbm = pl.BlockSpec(memory_space=pltpu.HBM)
        late = [i for i, o in enumerate(operands) if o is not at and i not in near]
        leaving = [i for i in range(len(outs)) if i not in kept]

        def kernel(*refs):
            n_in, n_out = len(operands), len(outs)
            ins, results = list(refs[:n_in]), list(refs[n_in : n_in + n_out])
            rest = list(refs[n_in + n_out :])
            in_bufs, rest = rest[: len(late)], rest[len(late) :]
            out_bufs, rest = rest[: len(leaving)], rest[len(leaving) :]
            in_sems, out_sems, rest = rest[0], rest[1], rest[2:]
            for k, i in enumerate(late):
                source = views[i][1](ins[i], ins[0]) if i in views else ins[i]
                ins[i] = Late(pltpu.make_async_copy(source, in_bufs[k], in_sems.at[k]), in_bufs[k])
            for k, i in enumerate(leaving):
                results[i] = Leaving(
                    pltpu.make_async_copy(out_bufs[k], results[i], out_sems.at[k]), out_bufs[k]
                )
            body(*ins, *results, *rest)
            for i in late:
                ins[i].ready()
            for i in leaving:
                results[i].copy.wait()

        return pl.pallas_call(
            kernel,
            out_shape=outs,
            in_specs=[
                pl.BlockSpec(memory_space=pltpu.SMEM) if o is at else hbm if i in late else vmem
                for i, o in enumerate(operands)
            ],
            out_specs=[hbm if i in leaving else vmem for i in range(len(outs))],
            scratch_shapes=[
                pltpu.VMEM(views[i][0] if i in views else operands[i].shape, operands[i].dtype)
                for i in late
            ]
            + [pltpu.VMEM(outs[i].shape, outs[i].dtype) for i in leaving]
            + [
                pltpu.SemaphoreType.DMA((max(len(late), 1),)),
                pltpu.SemaphoreType.DMA((max(len(leaving), 1),)),
            ]
            + list(scratch),
            compiler_params=pltpu.CompilerParams(vmem_limit_bytes=64 * MIB),
            cost_estimate=pl.CostEstimate(flops=flops, bytes_accessed=0, transcendentals=0),
        )(*operands)

    def up_rows(flip):
        def cut(ref, at_ref):
            return ref.at[pl.ds(pl.multiple_of((at_ref[1] ^ flip) * half, LANES), half), :]

        return ((half, hid), cut)

    send, base, placed = run(
        functools.partial(pack_kernel, capacity, n_experts, n_clips),
        [
            sds((n_experts, 2, capacity, half + LANES), bf16),
            sds((n_clips, width), f32),
            sds((tok_rows, n_experts * capacity), bf16),
        ],
        [routes.reshape(1, tok_rows), pool_ids, tokens],
        kept=(0, 1, 2),
    )
    recv = exchange(send.reshape(n_exp, capacity, half + LANES), "expert")
    start, _ = lax.optimization_barrier((captions, send))
    block = lax.ppermute(
        start,
        ("dp", "expert"),
        [(a * n_exp + b, (b * n_exp + a) if b < n_dp else a * n_exp + b) for a in range(n_dp) for b in range(n_exp)],
    )
    recv, block = lax.optimization_barrier((recv, block))
    other = lax.ppermute(recv, "expert", swap)
    gelu_slope, hidden, aux, counts, pay = run(
        functools.partial(forward_kernel, n_clips, strip),
        [
            sds((rows, hid), f32),
            sds((rows, hid), bf16),
            sds((rows, LANES), f32),
            sds((n_clips, LANES), f32),
            sds((n_exp // 2, 2, caps_dp, half + LANES), bf16),
        ],
        [at, recv, other, router_t, w_up, block, w_down, base],
        kept=(4,),
    )
    sums = exchange(pay.reshape(n_exp, caps_dp, half + LANES), "expert")
    (total,) = run(
        functools.partial(sum_kernel, strip),
        [sds((n_exp, n_clips, LANES), bf16)],
        [sums],
        kept=(0,),
        views={0: ((n_exp, caps_dp, LANES), lambda ref, _: ref.at[:, :, pl.ds(half, LANES)])},
    )
    total = exchange(total, "expert")
    other_sums = lax.ppermute(sums, "expert", swap)
    clip_grad, terms = run(
        functools.partial(loss_kernel, strip),
        [sds((n_clips, width), f32), sds((n_dp, caps_dp, LANES), f32)],
        [at, total, counts, sums, other_sums, clip_pairs.reshape(1, n_caps), teacher],
        near=(1,),
        scratch=[pltpu.VMEM((n_clips, width), f32)] * 3 + [pltpu.VMEM((n_caps, width), bf16)],
    )
    terms = exchange(terms, "dp")
    d_preact, dx_other, part = run(
        functools.partial(backward_kernel, n_clips),
        [sds((rows, hid), bf16), sds((rows, half), f32), sds((rows, LANES), f32)],
        [at, clip_grad, aux, w_down, gelu_slope, hidden, router_t, w_up],
        views={7: up_rows(1)},
        scratch=[pltpu.VMEM((rows + 2 * n_clips, width), bf16)],
    )
    from_other = lax.ppermute(dx_other, "expert", swap)
    (dx_own,) = run(
        own_kernel,
        [sds((rows, half), f32)],
        [at, d_preact, w_up, part, router_t],
        views={2: up_rows(0)},
        flops=COVER,
    )
    (pay,) = run(
        return_kernel,
        [sds((n_exp, capacity, half + LANES), bf16)],
        [dx_own, from_other, terms],
        kept=(0,),
    )
    back = exchange(pay, "expert")
    members = (pool_ids[0][:, None] == jnp.arange(n_clips, dtype=jnp.int32)[None, :]).astype(f32)
    token_dy = jnp.dot(members, clip_grad, precision=HIGHEST)
    token_grads, caption_grads = run(
        functools.partial(final_kernel, strip),
        [sds((tok_rows, width), f32), sds((caps_dp, width), f32)],
        [back.reshape(n_experts, 2, capacity, half + LANES), placed, token_dy],
        near=(0, 1, 2),
        kept=(0, 1),
    )
    return (token_grads, caption_grads)


def solution(mesh):
    return jax.shard_map(
        shards,
        mesh=mesh,
        in_specs=(
            P(("dp", "expert"), None),
            P(("dp", "expert"), None),
            P("dp", "expert"),
            P(),
            P(None, "expert"),
            P("expert", None),
            P("dp", None),
            P(),
            P("dp", None),
        ),
        out_specs=(P(("dp", "expert"), None), P("dp", None)),
        check_vma=False,
    )
```

```python
import functools
import jax
import jax.numpy as jnp
from jax import lax
from jax.experimental import pallas as pl
from jax.experimental.pallas import tpu as pltpu
from jax.sharding import PartitionSpec as P

HIGHEST = lax.Precision.HIGHEST
logit_scale = 10.0
logit_shift = -10.0
norm_eps = 1e-06
f32 = jnp.float32
bf16 = jnp.bfloat16
LANES = 128
MIB = 1 << 20
COVER = 10_000_000_000


def exchange(x, axis):
    return lax.all_to_all(x, axis, split_axis=0, concat_axis=0, tiled=True)


class Late:
    def __init__(self, copy, ref):
        self.copy, self.ref, self.waited = copy, ref, False
        copy.start()

    def ready(self):
        if not self.waited:
            self.copy.wait()
            self.waited = True
        return self.ref


class Leaving:
    def __init__(self, copy, ref):
        self.copy, self.ref, self.sent = copy, ref, False

    def send(self, value):
        self.ref[...] = value
        self.copy.start()
        self.sent = True


def iota(shape, axis):
    return lax.broadcasted_iota(jnp.int32, shape, axis)


def nn(a, b):
    return lax.dot_general(a, b, (((1,), (0,)), ((), ())), preferred_element_type=f32)


def nt(a, b):
    return lax.dot_general(a, b, (((1,), (1,)), ((), ())), preferred_element_type=f32)


def stack3(x):
    high = x.astype(bf16).astype(f32)
    rest = x - high
    mid = rest.astype(bf16).astype(f32)
    return jnp.concatenate([high, mid, rest - mid], axis=0).astype(bf16)


def fold3(x):
    rows = x.shape[0] // 3
    return x[:rows] + (x[rows : 2 * rows] + x[2 * rows :])


def slot_matrix(route_row, capacity, n_experts):
    toks = route_row.shape[1]
    chosen = (iota((n_experts, toks), 0) == route_row).astype(f32)
    earlier = (iota((toks, toks), 0) < iota((toks, toks), 1)).astype(f32).astype(bf16)
    before = nn(chosen.astype(bf16), earlier)
    arrival = jnp.sum(before * chosen, axis=0, keepdims=True)
    slot = route_row.astype(f32) * capacity + arrival
    slot = jnp.where(arrival < capacity, slot, -1.0)
    return (iota((n_experts * capacity, toks), 0).astype(f32) == slot).astype(f32)


def pack_kernel(capacity, n_experts, n_clips, route, pool, tok, send_ref, base_ref, placed_ref):
    toks, width = tok.ref.shape
    half = width // 2
    placed_t = slot_matrix(route.ready()[...], capacity, n_experts)
    placed_ref[...] = placed_t.T.astype(bf16)
    placed_t = placed_t.astype(bf16)
    pool = pool.ready()[...]
    ids = iota((LANES, toks), 0)
    members = (ids == pool).astype(f32)
    counted = (ids - n_clips == pool).astype(f32).astype(bf16)
    side = nt(placed_t, members.astype(bf16)) + nt(
        jnp.ones((n_experts * capacity, toks), bf16), counted
    )
    side = side.reshape(n_experts, capacity, LANES).astype(bf16)
    tokens = tok.ready()[...]
    rows = nn(placed_t, tokens)
    for h in range(2):
        send_ref[:, h, :, :half] = (
            rows[:, h * half : (h + 1) * half].reshape(n_experts, capacity, half).astype(bf16)
        )
        send_ref[:, h, :, half:] = side
    base_ref[...] = nn(members[:n_clips].astype(bf16), tokens)


def cut_strip(tiles, e, strip):
    tile, offset = divmod(e * strip, LANES)
    lane = iota(tiles[0].shape, 1)
    value = tiles[tile]
    if offset + strip > LANES:
        value = jnp.where(lane >= offset, value, tiles[tile + 1])
    if offset:
        value = pltpu.roll(value, LANES - offset, 1)
    return jnp.where(lane < strip, value, 0.0)


def join_strips(strips, strip, n_tiles):
    lane = iota(strips[0].shape, 1)
    tiles = [jnp.zeros(strips[0].shape, f32) for _ in range(n_tiles)]
    for e, value in enumerate(strips):
        tile, offset = divmod(e * strip, LANES)
        if offset:
            value = pltpu.roll(value, offset, 1)
        if offset + strip > LANES:
            tiles[tile] = tiles[tile] + jnp.where(lane >= offset, value, 0.0)
            tiles[tile + 1] = tiles[tile + 1] + jnp.where(lane < offset, value, 0.0)
        else:
            tiles[tile] = tiles[tile] + value
    return tiles


def spread3(value, strip):
    high = value.astype(bf16).astype(f32)
    rest = value - high
    mid = rest.astype(bf16).astype(f32)
    return high + pltpu.roll(mid, strip, 1) + pltpu.roll(rest - mid, 2 * strip, 1)


def gather3(value, strip):
    lane = iota(value.shape, 1)
    low = pltpu.roll(value, LANES - 2 * strip, 1)
    mid = pltpu.roll(value, LANES - strip, 1)
    return jnp.where(lane < strip, value + (mid + low), 0.0)


def first_kernel(at_ref, recv, up, out):
    n_exp, capacity, half = recv.ref.shape
    own = recv.ready()[...].astype(f32).reshape(n_exp * capacity, half).astype(bf16)
    out.send(nn(own, up.ready()[...]))


def forward_kernel(
    n_clips, strip, at_ref, recv, other, router, up, partial, block, down, base,
    slope, hidden_out, aux_out, counts, pay_ref,
):
    n_exp, capacity, wide = recv.ref.shape
    half = wide - LANES
    rows = n_exp * capacity
    n_experts = router.ref.shape[0]
    expert = at_ref[0]
    own_at = pl.multiple_of(at_ref[1] * half, LANES)
    other_at = pl.multiple_of((1 - at_ref[1]) * half, LANES)
    recv_ref = recv.ready()
    own = recv_ref[:, :, :half].astype(f32).reshape(rows, half).astype(bf16)
    side = recv_ref[:, :, half:].astype(f32).reshape(rows, LANES)
    other_rows = other.ready()[:, :, :half].astype(f32).reshape(rows, half).astype(bf16)
    router_ref = router.ready()
    scores = nt(own, router_ref[:, pl.ds(own_at, half)]) + nt(
        other_rows, router_ref[:, pl.ds(other_at, half)]
    )
    mine = iota((rows, n_experts), 1) == expert
    score = jnp.sum(jnp.where(mine, scores, 0.0), axis=1, keepdims=True)
    sigmoid_gate = jax.nn.sigmoid(score)
    gate = sigmoid_gate.astype(bf16).astype(f32)
    lane = iota((rows, LANES), 1)
    clip = jnp.where(lane < n_clips, side, 0.0)
    aux_out.send(
        jnp.where(
            lane == n_clips,
            gate,
            jnp.where(lane == n_clips + 1, sigmoid_gate * (1.0 - sigmoid_gate), clip),
        )
    )
    side_t = side.T
    counts.send(
        jnp.broadcast_to(
            jnp.sum(side_t[n_clips : 2 * n_clips], axis=1, keepdims=True) / capacity,
            (n_clips, LANES),
        )
    )
    weights = (clip * gate).T[:n_clips].astype(bf16)
    preact = nn(other_rows, up.ready()[...]) + partial.ready()[...]
    root = 0.7978845608028654
    square = preact * preact
    tanh = jnp.tanh(root * (preact + 0.044715 * (square * preact)))
    hidden = (preact * (0.5 * (1.0 + tanh))).astype(bf16)
    hidden_out.send(hidden)
    slope.send(
        0.5 * (1.0 + tanh)
        + 0.5 * preact * (1.0 - tanh * tanh) * (root * (1.0 + (3 * 0.044715) * square))
    )
    captions = block.ready()
    for h in range(2):
        pay_ref[:, h, :, :half] = jnp.broadcast_to(
            captions[:, h * half : (h + 1) * half][None], (n_exp // 2, captions.shape[0], half)
        )
    produced = nn(hidden, down.ready()[...])
    high = produced.astype(bf16)
    low = (produced - high.astype(f32)).astype(bf16)
    pooled = base.ready()[...] + (nn(weights, high) + nn(weights, low))
    tiles = [pooled[:, t * LANES : (t + 1) * LANES] for t in range(pooled.shape[1] // LANES)]
    for e in range(n_exp):
        pay_ref[e // 2, e % 2, :, half:] = spread3(cut_strip(tiles, e, strip), strip).astype(bf16)


def sum_kernel(strip, side, out_ref):
    total = jnp.sum(side.ready()[...].astype(f32), axis=0)
    total = spread3(gather3(total, strip), strip).astype(bf16)
    out_ref[...] = jnp.broadcast_to(total[None], out_ref.shape)


def loss_kernel(
    strip, at_ref, sums_ref, counts, own, other, pairs, teacher, grad_out, terms_out,
    mean_ref, image_ref, d_image_ref, text_ref,
):
    n_exp, n_clips, wide = own.ref.shape
    n_caps = teacher.ref.shape[1]
    half = wide - LANES
    width = 2 * half
    own_at = pl.multiple_of(at_ref[1] * half, LANES)
    other_at = pl.multiple_of((1 - at_ref[1]) * half, LANES)
    own_dp = at_ref[2]
    n_tiles = width // LANES
    tiles = join_strips(
        [gather3(sums_ref[e].astype(f32), strip) for e in range(n_exp)], strip, n_tiles
    )
    counts = counts.ready()[:, :1]
    for t, tile in enumerate(tiles):
        mean_ref[:, t * LANES : (t + 1) * LANES] = tile / counts
    clip_mean = mean_ref[...]
    img_scale = lax.rsqrt(jnp.sum(clip_mean * clip_mean, axis=1, keepdims=True) + norm_eps)
    image_emb = clip_mean * img_scale
    image_ref[...] = image_emb
    own_text = own.ready()[:, :, :half].astype(f32).reshape(n_caps, half)
    other_text = other.ready()[:, :, :half].astype(f32).reshape(n_caps, half)
    ones = jnp.ones((16, half), bf16)

    def squares(text):
        square = text * text
        high = square.astype(bf16)
        return nt(ones, high) + nt(ones, (square - high.astype(f32)).astype(bf16))

    text_scale = lax.rsqrt((squares(own_text) + squares(other_text))[:n_clips] + norm_eps)
    own_text = own_text.astype(bf16)
    other_text = other_text.astype(bf16)
    text_ref[:, pl.ds(own_at, half)] = own_text
    text_ref[:, pl.ds(other_at, half)] = other_text
    text = text_ref[...]
    raw = fold3(nt(stack3(image_emb), text))
    matched = (
        pairs.ready()[...] == own_dp * n_clips + iota((n_clips, n_caps), 0)
    ).astype(f32)
    target = 0.5 * matched + 0.5 * jax.nn.sigmoid(teacher.ready()[...])
    logits = logit_scale * raw * text_scale + logit_shift
    loss_grad = (jax.nn.sigmoid(logits) - target) * (counts / n_caps)
    scaled = loss_grad * text_scale
    d_image = logit_scale * fold3(nn(stack3(scaled), text))
    mean_grad = (
        img_scale * d_image
        - img_scale
        * img_scale
        * img_scale
        * jnp.sum(clip_mean * d_image, axis=1, keepdims=True)
        * clip_mean
    )
    grad_out.send(mean_grad / counts)
    pick = (
        (iota((width, LANES), 0) - at_ref[3] * strip == iota((width, LANES), 1))
        & (iota((width, LANES), 1) < strip)
    ).astype(f32).astype(bf16)
    emb_strip = fold3(nn(stack3(image_emb), pick))
    raw_strip = nn(text, pick)
    dots = jnp.sum(loss_grad * raw, axis=0, keepdims=True)
    cube = text_scale[:1] * text_scale[:1] * text_scale[:1] * dots
    both = jnp.concatenate([scaled, jnp.broadcast_to(cube, scaled.shape)], axis=0)
    both = jnp.concatenate([both, jnp.zeros((LANES - both.shape[0], n_caps), f32)], axis=0).T
    products = lax.dot_general(
        both[:, :n_clips], emb_strip, (((1,), (0,)), ((), ())),
        precision=HIGHEST, preferred_element_type=f32,
    )
    terms = logit_scale * (products - both[:, n_clips : n_clips + 1] * raw_strip)
    terms_out.send(terms.reshape(terms_out.ref.shape))


def backward_kernel(
    n_clips, at_ref, grad, aux, down, slope, hidden, router, up,
    d_preact_out, out, part_out, stacked_ref,
):
    rows, hid = hidden.ref.shape
    width = grad.ref.shape[1]
    half = width // 2
    expert = at_ref[0]
    other_at = pl.multiple_of((1 - at_ref[1]) * half, LANES)
    grads = grad.ready()[...]
    aux = aux.ready()[...]
    lane = iota((rows, LANES), 1)
    clip = jnp.sum(jnp.where(lane < n_clips, aux * lane.astype(f32), 0.0), axis=1, keepdims=True)
    gate = aux[:, n_clips : n_clips + 1]
    gate_slope = aux[:, n_clips + 1 : n_clips + 2]
    lane3 = lane % n_clips
    thrice = ((lane3.astype(f32) == clip) & (lane < 3 * n_clips)).astype(f32).astype(bf16)
    high = grads.astype(bf16).astype(f32)
    rest = grads - high
    mid = rest.astype(bf16).astype(f32)
    parts = jnp.concatenate(
        [high, mid, rest - mid, jnp.zeros((LANES - 3 * n_clips, width), f32)], axis=0
    ).astype(bf16)
    unit_dy = nn(thrice, parts)
    stacked_ref[:rows, :] = (gate * unit_dy).astype(bf16)
    stacked_ref[rows:, :] = jnp.concatenate([high, mid], axis=0).astype(bf16)
    d_all = nt(stacked_ref[...], down.ready()[...])
    d_preact = (d_all[:rows] * slope.ready()[...]).astype(bf16)
    d_preact_out.send(d_preact)
    by_clip = d_all[rows : rows + n_clips] + d_all[rows + n_clips :]
    high_v = by_clip.astype(bf16).astype(f32)
    two = jnp.concatenate([high_v, by_clip - high_v], axis=0).astype(bf16)
    dots = nt(hidden.ready()[...], two)
    lane2 = iota((rows, 2 * n_clips), 1) % n_clips
    token_dg = jnp.sum(
        jnp.where(lane2.astype(f32) == clip, dots, 0.0), axis=1, keepdims=True
    )
    part = token_dg * gate_slope
    part_out.send(jnp.broadcast_to(part, (rows, LANES)))
    router = jnp.sum(
        jnp.where(
            iota((router.ref.shape[0], half), 0) == expert,
            router.ready()[:, pl.ds(other_at, half)].astype(f32),
            0.0,
        ),
        axis=0,
        keepdims=True,
    )
    out.send(nt(d_preact, up.ready()[...]) + part * router)


def own_kernel(at_ref, d_preact, up, part, router, out):
    half = out.ref.shape[1]
    expert = at_ref[0]
    own_at = pl.multiple_of(at_ref[1] * half, LANES)
    router = jnp.sum(
        jnp.where(
            iota((router.ref.shape[0], half), 0) == expert,
            router.ready()[:, pl.ds(own_at, half)].astype(f32),
            0.0,
        ),
        axis=0,
        keepdims=True,
    )
    out.send(
        nt(d_preact.ready()[...], up.ready()[...])
        + part.ready()[:, :1] * router
    )


def return_kernel(own, other, terms, pay_ref):
    n_exp, capacity, _ = pay_ref.shape
    half = own.ref.shape[1]
    strip = jnp.sum(terms.ready()[...], axis=0)
    strip_high = strip.astype(bf16).astype(f32)
    side = strip_high + pltpu.roll(strip - strip_high, LANES // 2, 1)
    pay_ref[:, :, half:] = jnp.broadcast_to(
        side.astype(bf16)[None], (n_exp, capacity, LANES)
    )
    total = (own.ready()[...] + other.ready()[...]).reshape(n_exp, capacity, half)
    pay_ref[:, :, :half] = total.astype(bf16)


def final_kernel(strip, back_ref, placed_ref, dy_ref, out_ref, caps_ref):
    n_experts, _, capacity, wide = back_ref.shape
    half = wide - LANES
    placed = placed_ref[...]
    slots = n_experts * capacity

    for h in range(2):
        part = back_ref[:, h, :, :half].astype(f32).reshape(slots, half).astype(bf16)
        out_ref[:, h * half : (h + 1) * half] = (
            dy_ref[:, h * half : (h + 1) * half] + nn(placed, part)
        )
    lane = iota((capacity, LANES), 1)
    strips = []
    for e in range(2 * n_experts):
        side = back_ref[e // 2, e % 2, :, half:].astype(f32)
        strips.append(jnp.where(lane < strip, side + pltpu.roll(side, LANES // 2, 1), 0.0))
    for t, value in enumerate(join_strips(strips, strip, caps_ref.shape[1] // LANES)):
        caps_ref[:, t * LANES : (t + 1) * LANES] = value


def shards(tokens, routes, pool_ids, w_router, w_up, w_down, captions, clip_pairs, teacher):
    tok_rows, width = tokens.shape
    n_experts = w_router.shape[1]
    n_clips, n_caps = teacher.shape
    hid = w_up.shape[1]
    n_dp = lax.axis_size("dp")
    n_exp = lax.axis_size("expert")
    caps_dp = n_caps // n_dp
    capacity = tok_rows // n_experts
    half = width // 2
    strip = width // n_exp
    rows = n_exp * capacity
    own = lax.axis_index("expert")
    own_dp = lax.axis_index("dp")
    at = jnp.stack([own // 2, own % 2, own_dp, own]).astype(jnp.int32)
    swap = [(i, i ^ 1) for i in range(n_exp)]
    router_t = w_router.T
    sds = jax.ShapeDtypeStruct

    def run(body, outs, operands, near=(), kept=(), views=(), scratch=(), flops=0):
        views = dict(views)
        vmem = pl.BlockSpec(memory_space=pltpu.VMEM)
        hbm = pl.BlockSpec(memory_space=pltpu.HBM)
        late = [i for i, o in enumerate(operands) if o is not at and i not in near]
        leaving = [i for i in range(len(outs)) if i not in kept]

        def kernel(*refs):
            n_in, n_out = len(operands), len(outs)
            ins, results = list(refs[:n_in]), list(refs[n_in : n_in + n_out])
            rest = list(refs[n_in + n_out :])
            in_bufs, rest = rest[: len(late)], rest[len(late) :]
            out_bufs, rest = rest[: len(leaving)], rest[len(leaving) :]
            in_sems, out_sems, rest = rest[0], rest[1], rest[2:]
            for k, i in enumerate(late):
                source = views[i][1](ins[i], ins[0]) if i in views else ins[i]
                ins[i] = Late(pltpu.make_async_copy(source, in_bufs[k], in_sems.at[k]), in_bufs[k])
            for k, i in enumerate(leaving):
                results[i] = Leaving(
                    pltpu.make_async_copy(out_bufs[k], results[i], out_sems.at[k]), out_bufs[k]
                )
            body(*ins, *results, *rest)
            for i in late:
                ins[i].ready()
            for i in leaving:
                results[i].copy.wait()

        return pl.pallas_call(
            kernel,
            out_shape=outs,
            in_specs=[
                pl.BlockSpec(memory_space=pltpu.SMEM) if o is at else hbm if i in late else vmem
                for i, o in enumerate(operands)
            ],
            out_specs=[hbm if i in leaving else vmem for i in range(len(outs))],
            scratch_shapes=[
                pltpu.VMEM(views[i][0] if i in views else operands[i].shape, operands[i].dtype)
                for i in late
            ]
            + [pltpu.VMEM(outs[i].shape, outs[i].dtype) for i in leaving]
            + [
                pltpu.SemaphoreType.DMA((max(len(late), 1),)),
                pltpu.SemaphoreType.DMA((max(len(leaving), 1),)),
            ]
            + list(scratch),
            compiler_params=pltpu.CompilerParams(vmem_limit_bytes=64 * MIB),
            cost_estimate=pl.CostEstimate(flops=flops, bytes_accessed=0, transcendentals=0),
        )(*operands)

    def up_rows(flip):
        def cut(ref, at_ref):
            return ref.at[pl.ds(pl.multiple_of((at_ref[1] ^ flip) * half, LANES), half), :]

        return ((half, hid), cut)

    send, base, placed = run(
        functools.partial(pack_kernel, capacity, n_experts, n_clips),
        [
            sds((n_experts, 2, capacity, half + LANES), bf16),
            sds((n_clips, width), f32),
            sds((tok_rows, n_experts * capacity), bf16),
        ],
        [routes.reshape(1, tok_rows), pool_ids, tokens],
        kept=(0, 1, 2),
    )
    recv = exchange(send.reshape(n_exp, capacity, half + LANES), "expert")
    start, _ = lax.optimization_barrier((captions, send))
    block = lax.ppermute(
        start,
        ("dp", "expert"),
        [(a * n_exp + b, (b * n_exp + a) if b < n_dp else a * n_exp + b) for a in range(n_dp) for b in range(n_exp)],
    )
    recv, block = lax.optimization_barrier((recv, block))
    other = lax.ppermute(recv, "expert", swap)
    (partial,) = run(
        first_kernel,
        [sds((rows, hid), f32)],
        [at, recv, w_up],
        views={
            1: ((n_exp, capacity, half), lambda ref, _: ref.at[:, :, pl.ds(0, half)]),
            2: up_rows(0),
        },
        flops=2 * rows * half * hid,
    )
    gelu_slope, hidden, aux, counts, pay = run(
        functools.partial(forward_kernel, n_clips, strip),
        [
            sds((rows, hid), f32),
            sds((rows, hid), bf16),
            sds((rows, LANES), f32),
            sds((n_clips, LANES), f32),
            sds((n_exp // 2, 2, caps_dp, half + LANES), bf16),
        ],
        [at, recv, other, router_t, w_up, partial, block, w_down, base],
        kept=(4,),
        views={4: up_rows(1)},
    )
    sums = exchange(pay.reshape(n_exp, caps_dp, half + LANES), "expert")
    (total,) = run(
        functools.partial(sum_kernel, strip),
        [sds((n_exp, n_clips, LANES), bf16)],
        [sums],
        kept=(0,),
        views={0: ((n_exp, caps_dp, LANES), lambda ref, _: ref.at[:, :, pl.ds(half, LANES)])},
    )
    total = exchange(total, "expert")
    other_sums = lax.ppermute(sums, "expert", swap)
    clip_grad, terms = run(
        functools.partial(loss_kernel, strip),
        [sds((n_clips, width), f32), sds((n_dp, caps_dp, LANES), f32)],
        [at, total, counts, sums, other_sums, clip_pairs.reshape(1, n_caps), teacher],
        near=(1,),
        scratch=[pltpu.VMEM((n_clips, width), f32)] * 3 + [pltpu.VMEM((n_caps, width), bf16)],
    )
    terms = exchange(terms, "dp")
    d_preact, dx_other, part = run(
        functools.partial(backward_kernel, n_clips),
        [sds((rows, hid), bf16), sds((rows, half), f32), sds((rows, LANES), f32)],
        [at, clip_grad, aux, w_down, gelu_slope, hidden, router_t, w_up],
        views={7: up_rows(1)},
        scratch=[pltpu.VMEM((rows + 2 * n_clips, width), bf16)],
    )
    from_other = lax.ppermute(dx_other, "expert", swap)
    (dx_own,) = run(
        own_kernel,
        [sds((rows, half), f32)],
        [at, d_preact, w_up, part, router_t],
        views={2: up_rows(0)},
        flops=COVER,
    )
    (pay,) = run(
        return_kernel,
        [sds((n_exp, capacity, half + LANES), bf16)],
        [dx_own, from_other, terms],
        kept=(0,),
    )
    back = exchange(pay, "expert")
    members = (pool_ids[0][:, None] == jnp.arange(n_clips, dtype=jnp.int32)[None, :]).astype(f32)
    token_dy = jnp.dot(members, clip_grad, precision=HIGHEST)
    token_grads, caption_grads = run(
        functools.partial(final_kernel, strip),
        [sds((tok_rows, width), f32), sds((caps_dp, width), f32)],
        [back.reshape(n_experts, 2, capacity, half + LANES), placed, token_dy],
        near=(0, 1, 2),
        kept=(0, 1),
    )
    return (token_grads, caption_grads)


def solution(mesh):
    return jax.shard_map(
        shards,
        mesh=mesh,
        in_specs=(
            P(("dp", "expert"), None),
            P(("dp", "expert"), None),
            P("dp", "expert"),
            P(),
            P(None, "expert"),
            P("expert", None),
            P("dp", None),
            P(),
            P("dp", None),
        ),
        out_specs=(P(("dp", "expert"), None), P("dp", None)),
        check_vma=False,
    )
```

```python
import functools
import jax
import jax.numpy as jnp
from jax import lax
from jax.experimental import pallas as pl
from jax.experimental.pallas import tpu as pltpu
from jax.sharding import PartitionSpec as P

HIGHEST = lax.Precision.HIGHEST
logit_scale = 10.0
logit_shift = -10.0
norm_eps = 1e-06
f32 = jnp.float32
bf16 = jnp.bfloat16
LANES = 128
MIB = 1 << 20
COVER = 10_000_000_000


def exchange(x, axis):
    return lax.all_to_all(x, axis, split_axis=0, concat_axis=0, tiled=True)


class Late:
    def __init__(self, copy, ref):
        self.copy, self.ref, self.waited = copy, ref, False
        copy.start()

    def ready(self):
        if not self.waited:
            self.copy.wait()
            self.waited = True
        return self.ref


class Leaving:
    def __init__(self, copy, ref):
        self.copy, self.ref, self.sent = copy, ref, False

    def send(self, value):
        self.ref[...] = value
        self.copy.start()
        self.sent = True


def iota(shape, axis):
    return lax.broadcasted_iota(jnp.int32, shape, axis)


def nn(a, b):
    return lax.dot_general(a, b, (((1,), (0,)), ((), ())), preferred_element_type=f32)


def nt(a, b):
    return lax.dot_general(a, b, (((1,), (1,)), ((), ())), preferred_element_type=f32)


def stack3(x):
    high = x.astype(bf16).astype(f32)
    rest = x - high
    mid = rest.astype(bf16).astype(f32)
    return jnp.concatenate([high, mid, rest - mid], axis=0).astype(bf16)


def fold3(x):
    rows = x.shape[0] // 3
    return x[:rows] + (x[rows : 2 * rows] + x[2 * rows :])


def slot_matrix(route_row, capacity, n_experts):
    toks = route_row.shape[1]
    chosen = (iota((n_experts, toks), 0) == route_row).astype(f32)
    earlier = (iota((toks, toks), 0) < iota((toks, toks), 1)).astype(f32).astype(bf16)
    before = nn(chosen.astype(bf16), earlier)
    arrival = jnp.sum(before * chosen, axis=0, keepdims=True)
    slot = route_row.astype(f32) * capacity + arrival
    slot = jnp.where(arrival < capacity, slot, -1.0)
    return (iota((n_experts * capacity, toks), 0).astype(f32) == slot).astype(f32)


def pack_kernel(capacity, n_experts, n_clips, route, pool, tok, send_ref, base_ref, placed_ref):
    toks, width = tok.ref.shape
    half = width // 2
    placed_t = slot_matrix(route.ready()[...], capacity, n_experts)
    placed_ref[...] = placed_t.T.astype(bf16)
    placed_t = placed_t.astype(bf16)
    pool = pool.ready()[...]
    ids = iota((LANES, toks), 0)
    members = (ids == pool).astype(f32)
    counted = (ids - n_clips == pool).astype(f32).astype(bf16)
    side = nt(placed_t, members.astype(bf16)) + nt(
        jnp.ones((n_experts * capacity, toks), bf16), counted
    )
    side = side.reshape(n_experts, capacity, LANES).astype(bf16)
    tokens = tok.ready()[...]
    rows = nn(placed_t, tokens)
    for h in range(2):
        send_ref[:, h, :, :half] = (
            rows[:, h * half : (h + 1) * half].reshape(n_experts, capacity, half).astype(bf16)
        )
        send_ref[:, h, :, half:] = side
    base_ref[...] = nn(members[:n_clips].astype(bf16), tokens)


def cut_strip(tiles, e, strip):
    tile, offset = divmod(e * strip, LANES)
    lane = iota(tiles[0].shape, 1)
    value = tiles[tile]
    if offset + strip > LANES:
        value = jnp.where(lane >= offset, value, tiles[tile + 1])
    if offset:
        value = pltpu.roll(value, LANES - offset, 1)
    return jnp.where(lane < strip, value, 0.0)


def join_strips(strips, strip, n_tiles):
    lane = iota(strips[0].shape, 1)
    tiles = [jnp.zeros(strips[0].shape, f32) for _ in range(n_tiles)]
    for e, value in enumerate(strips):
        tile, offset = divmod(e * strip, LANES)
        if offset:
            value = pltpu.roll(value, offset, 1)
        if offset + strip > LANES:
            tiles[tile] = tiles[tile] + jnp.where(lane >= offset, value, 0.0)
            tiles[tile + 1] = tiles[tile + 1] + jnp.where(lane < offset, value, 0.0)
        else:
            tiles[tile] = tiles[tile] + value
    return tiles


def spread3(value, strip):
    high = value.astype(bf16).astype(f32)
    rest = value - high
    mid = rest.astype(bf16).astype(f32)
    return high + pltpu.roll(mid, strip, 1) + pltpu.roll(rest - mid, 2 * strip, 1)


def gather3(value, strip):
    lane = iota(value.shape, 1)
    low = pltpu.roll(value, LANES - 2 * strip, 1)
    mid = pltpu.roll(value, LANES - strip, 1)
    return jnp.where(lane < strip, value + (mid + low), 0.0)


def forward_kernel(
    n_clips, strip, at_ref, recv, other, router, up0, down0, up1, down1, block, base,
    slope, hidden_out, aux_out, counts, pay_ref,
):
    n_exp, capacity, wide = recv.ref.shape
    half = wide - LANES
    rows = n_exp * capacity
    n_experts = router.ref.shape[0]
    expert = at_ref[0]
    own_at = pl.multiple_of(at_ref[1] * half, LANES)
    other_at = pl.multiple_of((1 - at_ref[1]) * half, LANES)
    recv_ref = recv.ready()
    own = recv_ref[:, :, :half].astype(f32).reshape(rows, half).astype(bf16)
    side = recv_ref[:, :, half:].astype(f32).reshape(rows, LANES)
    other_rows = other.ready()[:, :, :half].astype(f32).reshape(rows, half).astype(bf16)
    router_ref = router.ready()
    scores = nt(own, router_ref[:, pl.ds(own_at, half)]) + nt(
        other_rows, router_ref[:, pl.ds(other_at, half)]
    )
    mine = iota((rows, n_experts), 1) == expert
    score = jnp.sum(jnp.where(mine, scores, 0.0), axis=1, keepdims=True)
    sigmoid_gate = jax.nn.sigmoid(score)
    gate = sigmoid_gate.astype(bf16).astype(f32)
    lane = iota((rows, LANES), 1)
    clip = jnp.where(lane < n_clips, side, 0.0)
    aux_out.send(
        jnp.where(
            lane == n_clips,
            gate,
            jnp.where(lane == n_clips + 1, sigmoid_gate * (1.0 - sigmoid_gate), clip),
        )
    )
    side_t = side.T
    counts.send(
        jnp.broadcast_to(
            jnp.sum(side_t[n_clips : 2 * n_clips], axis=1, keepdims=True) / capacity,
            (n_clips, LANES),
        )
    )
    weights = (clip * gate).T[:n_clips].astype(bf16)
    root = 0.7978845608028654
    produced = None
    part = up0.ref.shape[1]
    for c, (up, down) in enumerate(((up0, down0), (up1, down1))):
        up_ref = up.ready()
        preact = nn(own, up_ref[pl.ds(own_at, half), :]) + nn(
            other_rows, up_ref[pl.ds(other_at, half), :]
        )
        square = preact * preact
        tanh = jnp.tanh(root * (preact + 0.044715 * (square * preact)))
        hidden = (preact * (0.5 * (1.0 + tanh))).astype(bf16)
        hidden_out.ref[:, c * part : (c + 1) * part] = hidden
        slope.ref[:, c * part : (c + 1) * part] = 0.5 * (1.0 + tanh) + 0.5 * preact * (
            1.0 - tanh * tanh
        ) * (root * (1.0 + (3 * 0.044715) * square))
        more = nn(hidden, down.ready()[...])
        produced = more if produced is None else produced + more
    hidden_out.copy.start()
    slope.copy.start()
    captions = block.ready()
    for h in range(2):
        pay_ref[:, h, :, :half] = jnp.broadcast_to(
            captions[:, h * half : (h + 1) * half][None], (n_exp // 2, captions.shape[0], half)
        )
    high = produced.astype(bf16)
    low = (produced - high.astype(f32)).astype(bf16)
    pooled = base.ready()[...] + (nn(weights, high) + nn(weights, low))
    tiles = [pooled[:, t * LANES : (t + 1) * LANES] for t in range(pooled.shape[1] // LANES)]
    for e in range(n_exp):
        pay_ref[e // 2, e % 2, :, half:] = spread3(cut_strip(tiles, e, strip), strip).astype(bf16)


def sum_kernel(strip, side, out_ref):
    total = jnp.sum(side.ready()[...].astype(f32), axis=0)
    total = spread3(gather3(total, strip), strip).astype(bf16)
    out_ref[...] = jnp.broadcast_to(total[None], out_ref.shape)


def loss_kernel(
    strip, at_ref, sums_ref, counts, own, other, pairs, teacher, grad_out, terms_out,
    mean_ref, image_ref, d_image_ref, text_ref,
):
    n_exp, n_clips, wide = own.ref.shape
    n_caps = teacher.ref.shape[1]
    half = wide - LANES
    width = 2 * half
    own_at = pl.multiple_of(at_ref[1] * half, LANES)
    other_at = pl.multiple_of((1 - at_ref[1]) * half, LANES)
    own_dp = at_ref[2]
    n_tiles = width // LANES
    tiles = join_strips(
        [gather3(sums_ref[e].astype(f32), strip) for e in range(n_exp)], strip, n_tiles
    )
    counts = counts.ready()[:, :1]
    for t, tile in enumerate(tiles):
        mean_ref[:, t * LANES : (t + 1) * LANES] = tile / counts
    clip_mean = mean_ref[...]
    img_scale = lax.rsqrt(jnp.sum(clip_mean * clip_mean, axis=1, keepdims=True) + norm_eps)
    image_emb = clip_mean * img_scale
    image_ref[...] = image_emb
    own_text = own.ready()[:, :, :half].astype(f32).reshape(n_caps, half)
    other_text = other.ready()[:, :, :half].astype(f32).reshape(n_caps, half)
    ones = jnp.ones((16, half), bf16)

    def squares(text):
        square = text * text
        high = square.astype(bf16)
        return nt(ones, high) + nt(ones, (square - high.astype(f32)).astype(bf16))

    text_scale = lax.rsqrt((squares(own_text) + squares(other_text))[:n_clips] + norm_eps)
    own_text = own_text.astype(bf16)
    other_text = other_text.astype(bf16)
    text_ref[:, pl.ds(own_at, half)] = own_text
    text_ref[:, pl.ds(other_at, half)] = other_text
    text = text_ref[...]
    raw = fold3(nt(stack3(image_emb), text))
    matched = (
        pairs.ready()[...] == own_dp * n_clips + iota((n_clips, n_caps), 0)
    ).astype(f32)
    target = 0.5 * matched + 0.5 * jax.nn.sigmoid(teacher.ready()[...])
    logits = logit_scale * raw * text_scale + logit_shift
    loss_grad = (jax.nn.sigmoid(logits) - target) * (counts / n_caps)
    scaled = loss_grad * text_scale
    d_image = logit_scale * fold3(nn(stack3(scaled), text))
    mean_grad = (
        img_scale * d_image
        - img_scale
        * img_scale
        * img_scale
        * jnp.sum(clip_mean * d_image, axis=1, keepdims=True)
        * clip_mean
    )
    grad_out.send(mean_grad / counts)
    pick = (
        (iota((width, LANES), 0) - at_ref[3] * strip == iota((width, LANES), 1))
        & (iota((width, LANES), 1) < strip)
    ).astype(f32).astype(bf16)
    emb_strip = fold3(nn(stack3(image_emb), pick))
    raw_strip = nn(text, pick)
    dots = jnp.sum(loss_grad * raw, axis=0, keepdims=True)
    cube = text_scale[:1] * text_scale[:1] * text_scale[:1] * dots
    both = jnp.concatenate([scaled, jnp.broadcast_to(cube, scaled.shape)], axis=0)
    both = jnp.concatenate([both, jnp.zeros((LANES - both.shape[0], n_caps), f32)], axis=0).T
    products = lax.dot_general(
        both[:, :n_clips], emb_strip, (((1,), (0,)), ((), ())),
        precision=HIGHEST, preferred_element_type=f32,
    )
    terms = logit_scale * (products - both[:, n_clips : n_clips + 1] * raw_strip)
    terms_out.send(terms.reshape(terms_out.ref.shape))


def backward_kernel(
    n_clips, at_ref, grad, aux, down, slope, hidden, router, up,
    d_preact_out, out, part_out, stacked_ref,
):
    rows, hid = hidden.ref.shape
    width = grad.ref.shape[1]
    half = width // 2
    expert = at_ref[0]
    other_at = pl.multiple_of((1 - at_ref[1]) * half, LANES)
    grads = grad.ready()[...]
    aux = aux.ready()[...]
    lane = iota((rows, LANES), 1)
    clip = jnp.sum(jnp.where(lane < n_clips, aux * lane.astype(f32), 0.0), axis=1, keepdims=True)
    gate = aux[:, n_clips : n_clips + 1]
    gate_slope = aux[:, n_clips + 1 : n_clips + 2]
    lane3 = lane % n_clips
    thrice = ((lane3.astype(f32) == clip) & (lane < 3 * n_clips)).astype(f32).astype(bf16)
    high = grads.astype(bf16).astype(f32)
    rest = grads - high
    mid = rest.astype(bf16).astype(f32)
    parts = jnp.concatenate(
        [high, mid, rest - mid, jnp.zeros((LANES - 3 * n_clips, width), f32)], axis=0
    ).astype(bf16)
    unit_dy = nn(thrice, parts)
    stacked_ref[:rows, :] = (gate * unit_dy).astype(bf16)
    stacked_ref[rows:, :] = jnp.concatenate([high, mid], axis=0).astype(bf16)
    d_all = nt(stacked_ref[...], down.ready()[...])
    d_preact = (d_all[:rows] * slope.ready()[...]).astype(bf16)
    d_preact_out.send(d_preact)
    by_clip = d_all[rows : rows + n_clips] + d_all[rows + n_clips :]
    high_v = by_clip.astype(bf16).astype(f32)
    two = jnp.concatenate([high_v, by_clip - high_v], axis=0).astype(bf16)
    dots = nt(hidden.ready()[...], two)
    lane2 = iota((rows, 2 * n_clips), 1) % n_clips
    token_dg = jnp.sum(
        jnp.where(lane2.astype(f32) == clip, dots, 0.0), axis=1, keepdims=True
    )
    part = token_dg * gate_slope
    part_out.send(jnp.broadcast_to(part, (rows, LANES)))
    router = jnp.sum(
        jnp.where(
            iota((router.ref.shape[0], half), 0) == expert,
            router.ready()[:, pl.ds(other_at, half)].astype(f32),
            0.0,
        ),
        axis=0,
        keepdims=True,
    )
    out.send(nt(d_preact, up.ready()[...]) + part * router)


def own_kernel(at_ref, d_preact, up, part, router, out):
    half = out.ref.shape[1]
    expert = at_ref[0]
    own_at = pl.multiple_of(at_ref[1] * half, LANES)
    router = jnp.sum(
        jnp.where(
            iota((router.ref.shape[0], half), 0) == expert,
            router.ready()[:, pl.ds(own_at, half)].astype(f32),
            0.0,
        ),
        axis=0,
        keepdims=True,
    )
    out.send(
        nt(d_preact.ready()[...], up.ready()[...])
        + part.ready()[:, :1] * router
    )


def return_kernel(own, other, terms, pay_ref):
    n_exp, capacity, _ = pay_ref.shape
    half = own.ref.shape[1]
    strip = jnp.sum(terms.ready()[...], axis=0)
    strip_high = strip.astype(bf16).astype(f32)
    side = strip_high + pltpu.roll(strip - strip_high, LANES // 2, 1)
    pay_ref[:, :, half:] = jnp.broadcast_to(
        side.astype(bf16)[None], (n_exp, capacity, LANES)
    )
    total = (own.ready()[...] + other.ready()[...]).reshape(n_exp, capacity, half)
    pay_ref[:, :, :half] = total.astype(bf16)


def final_kernel(strip, back_ref, placed_ref, dy_ref, out_ref, caps_ref):
    n_experts, _, capacity, wide = back_ref.shape
    half = wide - LANES
    placed = placed_ref[...]
    slots = n_experts * capacity

    for h in range(2):
        part = back_ref[:, h, :, :half].astype(f32).reshape(slots, half).astype(bf16)
        out_ref[:, h * half : (h + 1) * half] = (
            dy_ref[:, h * half : (h + 1) * half] + nn(placed, part)
        )
    lane = iota((capacity, LANES), 1)
    strips = []
    for e in range(2 * n_experts):
        side = back_ref[e // 2, e % 2, :, half:].astype(f32)
        strips.append(jnp.where(lane < strip, side + pltpu.roll(side, LANES // 2, 1), 0.0))
    for t, value in enumerate(join_strips(strips, strip, caps_ref.shape[1] // LANES)):
        caps_ref[:, t * LANES : (t + 1) * LANES] = value


def shards(tokens, routes, pool_ids, w_router, w_up, w_down, captions, clip_pairs, teacher):
    tok_rows, width = tokens.shape
    n_experts = w_router.shape[1]
    n_clips, n_caps = teacher.shape
    hid = w_up.shape[1]
    n_dp = lax.axis_size("dp")
    n_exp = lax.axis_size("expert")
    caps_dp = n_caps // n_dp
    capacity = tok_rows // n_experts
    half = width // 2
    strip = width // n_exp
    rows = n_exp * capacity
    own = lax.axis_index("expert")
    own_dp = lax.axis_index("dp")
    at = jnp.stack([own // 2, own % 2, own_dp, own]).astype(jnp.int32)
    swap = [(i, i ^ 1) for i in range(n_exp)]
    router_t = w_router.T
    sds = jax.ShapeDtypeStruct

    def run(body, outs, operands, near=(), kept=(), views=(), scratch=(), flops=0):
        views = dict(views)
        vmem = pl.BlockSpec(memory_space=pltpu.VMEM)
        hbm = pl.BlockSpec(memory_space=pltpu.HBM)
        late = [i for i, o in enumerate(operands) if o is not at and i not in near]
        leaving = [i for i in range(len(outs)) if i not in kept]

        def kernel(*refs):
            n_in, n_out = len(operands), len(outs)
            ins, results = list(refs[:n_in]), list(refs[n_in : n_in + n_out])
            rest = list(refs[n_in + n_out :])
            in_bufs, rest = rest[: len(late)], rest[len(late) :]
            out_bufs, rest = rest[: len(leaving)], rest[len(leaving) :]
            in_sems, out_sems, rest = rest[0], rest[1], rest[2:]
            for k, i in enumerate(late):
                source = views[i][1](ins[i], ins[0]) if i in views else ins[i]
                ins[i] = Late(pltpu.make_async_copy(source, in_bufs[k], in_sems.at[k]), in_bufs[k])
            for k, i in enumerate(leaving):
                results[i] = Leaving(
                    pltpu.make_async_copy(out_bufs[k], results[i], out_sems.at[k]), out_bufs[k]
                )
            body(*ins, *results, *rest)
            for i in late:
                ins[i].ready()
            for i in leaving:
                results[i].copy.wait()

        return pl.pallas_call(
            kernel,
            out_shape=outs,
            in_specs=[
                pl.BlockSpec(memory_space=pltpu.SMEM) if o is at else hbm if i in late else vmem
                for i, o in enumerate(operands)
            ],
            out_specs=[hbm if i in leaving else vmem for i in range(len(outs))],
            scratch_shapes=[
                pltpu.VMEM(views[i][0] if i in views else operands[i].shape, operands[i].dtype)
                for i in late
            ]
            + [pltpu.VMEM(outs[i].shape, outs[i].dtype) for i in leaving]
            + [
                pltpu.SemaphoreType.DMA((max(len(late), 1),)),
                pltpu.SemaphoreType.DMA((max(len(leaving), 1),)),
            ]
            + list(scratch),
            compiler_params=pltpu.CompilerParams(vmem_limit_bytes=64 * MIB),
            cost_estimate=pl.CostEstimate(flops=flops, bytes_accessed=0, transcendentals=0),
        )(*operands)

    def up_rows(flip):
        def cut(ref, at_ref):
            return ref.at[pl.ds(pl.multiple_of((at_ref[1] ^ flip) * half, LANES), half), :]

        return ((half, hid), cut)

    send, base, placed = run(
        functools.partial(pack_kernel, capacity, n_experts, n_clips),
        [
            sds((n_experts, 2, capacity, half + LANES), bf16),
            sds((n_clips, width), f32),
            sds((tok_rows, n_experts * capacity), bf16),
        ],
        [routes.reshape(1, tok_rows), pool_ids, tokens],
        kept=(0, 1, 2),
    )
    recv = exchange(send.reshape(n_exp, capacity, half + LANES), "expert")
    start, _ = lax.optimization_barrier((captions, send))
    block = lax.ppermute(
        start,
        ("dp", "expert"),
        [(a * n_exp + b, (b * n_exp + a) if b < n_dp else a * n_exp + b) for a in range(n_dp) for b in range(n_exp)],
    )
    recv, block = lax.optimization_barrier((recv, block))
    other = lax.ppermute(recv, "expert", swap)
    gelu_slope, hidden, aux, counts, pay = run(
        functools.partial(forward_kernel, n_clips, strip),
        [
            sds((rows, hid), f32),
            sds((rows, hid), bf16),
            sds((rows, LANES), f32),
            sds((n_clips, LANES), f32),
            sds((n_exp // 2, 2, caps_dp, half + LANES), bf16),
        ],
        [at, recv, other, router_t, w_up, w_down, w_up, w_down, block, base],
        kept=(4,),
        views={
            i: (
                (width, hid // 2) if i % 2 == 0 else (hid // 2, width),
                lambda ref, _, i=i: ref.at[:, pl.ds((i - 4) // 2 * (hid // 2), hid // 2)]
                if i % 2 == 0
                else ref.at[pl.ds((i - 4) // 2 * (hid // 2), hid // 2), :],
            )
            for i in (4, 5, 6, 7)
        },
    )
    sums = exchange(pay.reshape(n_exp, caps_dp, half + LANES), "expert")
    (total,) = run(
        functools.partial(sum_kernel, strip),
        [sds((n_exp, n_clips, LANES), bf16)],
        [sums],
        kept=(0,),
        views={0: ((n_exp, caps_dp, LANES), lambda ref, _: ref.at[:, :, pl.ds(half, LANES)])},
    )
    total = exchange(total, "expert")
    other_sums = lax.ppermute(sums, "expert", swap)
    clip_grad, terms = run(
        functools.partial(loss_kernel, strip),
        [sds((n_clips, width), f32), sds((n_dp, caps_dp, LANES), f32)],
        [at, total, counts, sums, other_sums, clip_pairs.reshape(1, n_caps), teacher],
        near=(1,),
        scratch=[pltpu.VMEM((n_clips, width), f32)] * 3 + [pltpu.VMEM((n_caps, width), bf16)],
    )
    terms = exchange(terms, "dp")
    d_preact, dx_other, part = run(
        functools.partial(backward_kernel, n_clips),
        [sds((rows, hid), bf16), sds((rows, half), f32), sds((rows, LANES), f32)],
        [at, clip_grad, aux, w_down, gelu_slope, hidden, router_t, w_up],
        views={7: up_rows(1)},
        scratch=[pltpu.VMEM((rows + 2 * n_clips, width), bf16)],
    )
    from_other = lax.ppermute(dx_other, "expert", swap)
    (dx_own,) = run(
        own_kernel,
        [sds((rows, half), f32)],
        [at, d_preact, w_up, part, router_t],
        views={2: up_rows(0)},
        flops=COVER,
    )
    (pay,) = run(
        return_kernel,
        [sds((n_exp, capacity, half + LANES), bf16)],
        [dx_own, from_other, terms],
        kept=(0,),
    )
    back = exchange(pay, "expert")
    members = (pool_ids[0][:, None] == jnp.arange(n_clips, dtype=jnp.int32)[None, :]).astype(f32)
    token_dy = jnp.dot(members, clip_grad, precision=HIGHEST)
    token_grads, caption_grads = run(
        functools.partial(final_kernel, strip),
        [sds((tok_rows, width), f32), sds((caps_dp, width), f32)],
        [back.reshape(n_experts, 2, capacity, half + LANES), placed, token_dy],
        near=(0, 1, 2),
        kept=(0, 1),
    )
    return (token_grads, caption_grads)


def solution(mesh):
    return jax.shard_map(
        shards,
        mesh=mesh,
        in_specs=(
            P(("dp", "expert"), None),
            P(("dp", "expert"), None),
            P("dp", "expert"),
            P(),
            P(None, "expert"),
            P("expert", None),
            P("dp", None),
            P(),
            P("dp", None),
        ),
        out_specs=(P(("dp", "expert"), None), P("dp", None)),
        check_vma=False,
    )
```
